512 devices in a mesh: row: 8 (over x, core), col: 64 (over y, z).
Axes of the slice: x: 4, y: 4, z: 16, core: 2. Of those that a mesh axis runs over, the one named last changes fastest.
Arguments:
- teacher_tokens: bfloat16 [512, 8192], P('col', 'row'), may hold values from -6 to 6
- student_tokens: bfloat16 [512, 8192], P('col', 'row'), may hold values from -6 to 6
- gate_weight: bfloat16 [8192, 29568], P('row', 'col'), may hold values from -0.0625 to 0.0625
- up_weight: bfloat16 [8192, 29568], P('row', 'col'), may hold values from -0.0625 to 0.0625
- down_weight: bfloat16 [29568, 8192], P('col', 'row'), may hold values from -0.03125 to 0.03125
- expert_ids: int32 [512, 6], P('col'), may hold values from 0 to 63, as said below
- slot_ids: int32 [512, 6], P('col'), may hold values from 0 to 1, as said below
- route_weights: bfloat16 [512, 6], P('col'), may hold values from 1 to 8
Outputs:
- teacher_out: bfloat16 [512, 8192], P('col', 'row')
- student_out: bfloat16 [512, 8192], P('col', 'row')
- input_grad: bfloat16 [512, 8192], P('col', 'row')
The draws below stay inside these ranges and needn't reach their ends.
Inputs may be any that keep to these rules, and one draw needn't show every extreme that they name: `expert_ids`: each token names 6 different experts. Among the 8 tokens of one block no expert is named more than 2 times, and some expert is named exactly 2 times by every block. `slot_ids`: within one block of 8 tokens the choices of one expert carry different slots.
All inputs are finite; a program needn't handle non-finite values.
Results may differ from the reference program's by a relative error of at most 0.01.
Values may be sent and summed in bfloat16 or wider, within the bound.
A program may use at most 64 MiB of HBM per device.

```python
import math
import jax
import jax.numpy as jnp
from jax import lax

D = 8192
FF = 29568
TOPK = 6
TOK_COL = 8
TOKENS = 512
EXPERTS = 64
EH = 462
CAP = 2


def route_table(key):
    picks = TOK_COL * TOPK
    blocks = TOKENS // TOK_COL
    lowest = picks // CAP
    highest = min((picks + CAP - 2) // (CAP - 1) - 1, EXPERTS)
    bias_key, hot_key, score_key, count_key = jax.random.split(key, 4)
    bias = jax.random.randint(bias_key, (EXPERTS,), 0, 3) * 16384
    favored = jax.random.randint(hot_key, (), 0, EXPERTS)
    numbers = jnp.arange(EXPERTS, dtype=jnp.int32)
    bias = jnp.where(numbers == favored, 8 * 65536, bias)
    scores = (jax.random.randint(score_key, (blocks, EXPERTS), 0, 65536) + bias[None, :]) * EXPERTS + numbers[None, :]
    ranking = jnp.argsort(-scores, axis=1)
    counts = jax.random.randint(count_key, (blocks,), lowest, highest + 1)
    places = jnp.arange(picks, dtype=jnp.int32)
    column = places[None, :] % counts[:, None]
    chosen = jnp.take_along_axis(ranking, column, axis=1).astype(jnp.int32)
    slots = (places[None, :] // counts[:, None]).astype(jnp.int32)
    return (chosen.reshape(TOKENS, TOPK), slots.reshape(TOKENS, TOPK))


def draw_expert_ids(key, part):
    table = route_table(key)
    return table[0]


def draw_slot_ids(key, part):
    table = route_table(key)
    return table[1]


def steps_of(rng, shape, pieces, smallest, high):
    factor_of = 1.0
    for axis_at, shards_of in pieces:
        draws = jax.random.uniform(jax.random.fold_in(jax.random.fold_in(rng, 6), axis_at), (shards_of,), jnp.float32, smallest / len(pieces), high / len(pieces))
        factor_of = factor_of * jnp.repeat(jnp.exp(draws), shape[axis_at] // shards_of).reshape((-1,) + (1,) * (len(shape) - 1 - axis_at))
    return factor_of


def gaussian(stream_key, extent, width, reach, cuts=(), kind=jnp.bfloat16):
    result = jax.random.normal(stream_key, extent, jnp.float32) * width
    if len(cuts) > 0:
        result = steps_of(stream_key, extent, cuts, -0.22, 0.18) * result
    return jnp.clip(result, min=-reach, max=reach).astype(kind)


def setup_inputs(seed: int = 0) -> dict:
    seeds = jax.random.split(jax.random.key(seed), 9)
    return {
        "teacher_tokens": gaussian(seeds[0], (TOKENS, D), 1.0, 6.0, ((0, 64), (1, 8))),
        "student_tokens": gaussian(seeds[1], (TOKENS, D), 1.0, 6.0, ((0, 64), (1, 8))),
        "gate_weight": gaussian(seeds[2], (D, FF), D ** -0.5, 0.0625, ((0, 8), (1, 64))),
        "up_weight": gaussian(seeds[3], (D, FF), D ** -0.5, 0.0625, ((0, 8), (1, 64))),
        "down_weight": gaussian(seeds[4], (FF, D), FF ** -0.5, 0.03125, ((0, 64), (1, 8))),
        "expert_ids": draw_expert_ids(jax.random.fold_in(seeds[8], 71), 0),
        "slot_ids": draw_slot_ids(jax.random.fold_in(seeds[8], 71), 0),
        "route_weights": jnp.clip(jnp.exp(math.log(8.0) - 2.0794415 * jax.random.uniform(seeds[7], (TOKENS, TOPK), jnp.float32) ** steps_of(seeds[7], (TOKENS, TOPK), ((0, 64),), -0.2, 0.2)), 1.0, 8.0).astype(jnp.bfloat16),
    }


def silu_slope(value):
    logistic = jax.nn.sigmoid(value)
    return logistic * (1.0 + value * (1.0 - logistic))


def reference(teacher_tokens, student_tokens, gate_weight, up_weight, down_weight, expert_ids, slot_ids, route_weights):
    gate = jnp.dot(teacher_tokens, gate_weight, preferred_element_type=jnp.float32)
    upper = jnp.dot(teacher_tokens, up_weight, preferred_element_type=jnp.float32)
    hidden = (jax.nn.silu(gate) * upper).astype(jnp.bfloat16)
    teacher_out = jnp.dot(hidden, down_weight, preferred_element_type=jnp.float32).astype(jnp.bfloat16)

    blocks = TOKENS // TOK_COL
    source = (jnp.arange(TOKENS) // TOK_COL).astype(jnp.int32)
    source_rep = jnp.broadcast_to(source[:, None], (TOKENS, TOPK))
    spread_rows = jnp.broadcast_to(student_tokens[:, None, :], (TOKENS, TOPK, D))
    dispatched = jnp.zeros((EXPERTS, blocks, CAP, D), jnp.bfloat16)
    dispatched = dispatched.at[expert_ids, source_rep, slot_ids].set(spread_rows)

    def forward(index):
        rows = dispatched[index].reshape(blocks * CAP, D)
        gate_block = lax.dynamic_slice_in_dim(gate_weight, index * EH, EH, 1)
        up_block = lax.dynamic_slice_in_dim(up_weight, index * EH, EH, 1)
        down_block = lax.dynamic_slice_in_dim(down_weight, index * EH, EH, 0)
        pre_gate = jnp.dot(rows, gate_block, preferred_element_type=jnp.float32)
        pre_up = jnp.dot(rows, up_block, preferred_element_type=jnp.float32)
        activated = (jax.nn.silu(pre_gate) * pre_up).astype(jnp.bfloat16)
        produced = jnp.dot(activated, down_block, preferred_element_type=jnp.float32).astype(jnp.bfloat16)
        return pre_gate, pre_up, produced

    expert_index = jnp.arange(EXPERTS, dtype=jnp.int32)
    pre_gate, pre_up, expert_out = lax.map(forward, expert_index)
    expert_out = expert_out.reshape(EXPERTS, blocks, CAP, D)
    picked = expert_out[expert_ids, source_rep, slot_ids].astype(jnp.float32)
    weights = route_weights.astype(jnp.float32)
    student_out = jnp.sum(weights[:, :, None] * picked, axis=1).astype(jnp.bfloat16)

    loss_grad = (student_out.astype(jnp.float32) - teacher_out.astype(jnp.float32)).astype(jnp.bfloat16)
    slot_values = (weights[:, :, None] * loss_grad.astype(jnp.float32)[:, None, :]).astype(jnp.bfloat16)
    slot_grad = jnp.zeros((EXPERTS, blocks, CAP, D), jnp.bfloat16)
    slot_grad = slot_grad.at[expert_ids, source_rep, slot_ids].set(slot_values)

    def backward(index):
        rows = slot_grad[index].reshape(blocks * CAP, D)
        gate_block = lax.dynamic_slice_in_dim(gate_weight, index * EH, EH, 1)
        up_block = lax.dynamic_slice_in_dim(up_weight, index * EH, EH, 1)
        down_block = lax.dynamic_slice_in_dim(down_weight, index * EH, EH, 0)
        hidden_grad = jnp.dot(rows, down_block.T, preferred_element_type=jnp.float32)
        gate_grad = (hidden_grad * pre_up[index] * silu_slope(pre_gate[index])).astype(jnp.bfloat16)
        up_grad = (hidden_grad * jax.nn.silu(pre_gate[index])).astype(jnp.bfloat16)
        row_grad = jnp.dot(gate_grad, gate_block.T, preferred_element_type=jnp.float32)
        row_grad = row_grad + jnp.dot(up_grad, up_block.T, preferred_element_type=jnp.float32)
        return row_grad.astype(jnp.bfloat16)

    row_grad = lax.map(backward, expert_index).reshape(EXPERTS, blocks, CAP, D)
    picked_grad = row_grad[expert_ids, source_rep, slot_ids].astype(jnp.float32)
    input_grad = jnp.sum(picked_grad, axis=1).astype(jnp.bfloat16)
    return teacher_out, student_out, input_grad
```

```python
import functools

import jax
import jax.numpy as jnp
from jax import lax
from jax.experimental import pallas as pl
from jax.experimental.pallas import tpu as pltpu
from jax.sharding import PartitionSpec as P

MESH = pl.DeviceIdType.MESH
F32 = jnp.float32
BF16 = jnp.bfloat16

ROWS = 8
YS, ZS = 4, 16
COLS = YS * ZS
TOK = 8
WIDTH = 1024
LANES = 128
SUB = WIDTH // LANES
UNITS = 462
PAD = 512
CAP = 2
TOPK = 6
SLOTS = COLS * CAP
CHUNK = ZS * TOK
MINE = CHUNK // ROWS
BLOCK = TOK * SUB
MSG = CAP * SUB
SLOT_ROWS = COLS * MSG
STUDENT = YS
Y_OFFSETS = (0, 1, 3, 2)
TILE = 256


def dot(a, b):
    return jnp.dot(a, b, preferred_element_type=F32)


def dot_first(a, b):
    return lax.dot_general(a, b, (((0,), (0,)), ((), ())), preferred_element_type=F32)


def dot_last(a, b):
    return lax.dot_general(a, b, (((1,), (1,)), ((), ())), preferred_element_type=F32)


def to_lane_rows(rows):
    return jnp.concatenate([rows[:, j * LANES : (j + 1) * LANES] for j in range(SUB)], axis=0)


def from_lane_rows(block):
    return jnp.concatenate([block[j * TOK : (j + 1) * TOK, :] for j in range(SUB)], axis=1)


def kernel(
    teacher_ref,
    student_ref,
    gate_hbm,
    up_hbm,
    down_hbm,
    ids_ref,
    slots_ref,
    routes_ref,
    teacher_out,
    student_out,
    input_grad,
    gate_in,
    up_in,
    down_in,
    weight_sem,
    wide,
    down,
    tokens,
    placing,
    weighting,
    sent_slots,
    got_slots,
    spread,
    rows_in,
    part,
    part_got,
    hidden,
    pre,
    own_sum,
    y_send,
    y_got,
    z_send,
    z_got,
    back_send,
    back_got,
    loss_send,
    loss_got,
    hid_part,
    hid_got,
    grads,
    last_send,
    last_got,
    zg_send_sem,
    zg_recv_sem,
    yf_send_sem,
    yf_recv_sem,
    a2a_send_sem,
    a2a_recv_sem,
    rs_send_sem,
    rs_recv_sem,
    ag_send_sem,
    ag_recv_sem,
    yr_send_sem,
    yr_recv_sem,
    zr_send_sem,
    zr_recv_sem,
    ready_sem,
):
    r = lax.axis_index("row")
    c = lax.axis_index("col")
    x, core = r // 2, lax.rem(r, 2)
    y, z = c // ZS, lax.rem(c, ZS)

    def row_peer(m):
        return lax.rem(x + 1 + m // 2, 4) * 2 + lax.rem(core + 1 + lax.rem(m, 2), 2)

    def far_first(i):
        distance = ZS // 2 - (i + 1) // 2
        return lax.rem(z + distance * (1 - 2 * lax.rem(i + 1, 2)) + ZS, ZS)

    def col_peer(m):
        return lax.rem(y + 1 + lax.rem(m, YS), YS) * ZS + far_first(m // YS)

    def send(src, dst, send_sem, recv_sem, row, col):
        return pltpu.make_async_remote_copy(
            src_ref=src,
            dst_ref=dst,
            send_sem=send_sem,
            recv_sem=recv_sem,
            device_id=(row, col),
            device_id_type=MESH,
        )

    def wait_for(view, sem):
        pltpu.make_async_copy(view, view, sem).wait()

    weights = [
        pltpu.make_async_copy(a, b, weight_sem.at[i])
        for i, (a, b) in enumerate(((gate_hbm, gate_in), (up_hbm, up_in), (down_hbm, down_in)))
    ]
    for copy in weights:
        copy.start()
    barrier = pltpu.get_barrier_semaphore()

    @pl.loop(0, COLS - 1)
    def _(m):
        pl.semaphore_signal(barrier, inc=1, device_id=(r, col_peer(m)), device_id_type=MESH)

    @pl.loop(0, ROWS - 1)
    def _(m):
        pl.semaphore_signal(barrier, inc=1, device_id=(row_peer(m), c), device_id_type=MESH)

    tokens[c] = to_lane_rows(teacher_ref[...].astype(F32)).astype(BF16)
    targets = ids_ref[...] * CAP + slots_ref[...]
    routes = routes_ref[...].astype(F32)
    targets = jnp.concatenate([targets] * SUB, axis=0)
    routes = jnp.concatenate([routes] * SUB, axis=0)
    at = lax.broadcasted_iota(jnp.int32, (BLOCK, SLOT_ROWS), 1)
    lane_group = lax.broadcasted_iota(jnp.int32, (BLOCK, SLOT_ROWS), 0) // TOK
    slot_of = jnp.where(at % SUB == lane_group, at // SUB, -1)
    place = jnp.zeros((BLOCK, SLOT_ROWS), F32)
    weigh = jnp.zeros((BLOCK, SLOT_ROWS), F32)
    for k in range(TOPK):
        match = slot_of == targets[:, k : k + 1]
        place = jnp.where(match, 1.0, place)
        weigh = jnp.where(match, routes[:, k : k + 1], weigh)
    placing[...] = place.astype(BF16)
    weighting[...] = weigh.astype(BF16)
    student_rows = to_lane_rows(student_ref[...].astype(F32)).astype(BF16)
    sent_slots[...] = dot_first(placing[...], student_rows).astype(BF16)

    pl.semaphore_wait(barrier, COLS - 1 + ROWS - 1)

    def gather_z(i):
        to = y * ZS + far_first(i)
        return send(tokens.at[c], tokens.at[c], zg_send_sem, zg_recv_sem.at[z], r, to)

    @pl.loop(0, ZS - 1)
    def _(i):
        gather_z(i).start()

    def forward_y(zi):
        block = tokens.at[y * ZS + zi]
        for o in (2, 1, 3):
            to = lax.rem(y + o, YS) * ZS + z
            send(block, block, yf_send_sem, yf_recv_sem.at[YS - o], r, to).start()

    forward_y(z)

    def all_to_all(n, src, dst):
        @pl.loop(0, COLS - 1)
        def _(m):
            to = col_peer(m)
            send(
                src.at[pl.ds(pl.multiple_of(to * MSG, MSG), MSG)],
                dst.at[pl.ds(pl.multiple_of(c * MSG, MSG), MSG)],
                a2a_send_sem.at[n],
                a2a_recv_sem.at[n],
                r,
                to,
            ).start()

        own = pl.ds(pl.multiple_of(c * MSG, MSG), MSG)
        dst[own, :] = src[own, :]

    def all_to_all_wait(n, src, dst):
        most = pl.ds(0, (COLS - 1) * MSG)
        wait_for(dst.at[most], a2a_recv_sem.at[n])

    def all_to_all_done(n, src):
        most = pl.ds(0, (COLS - 1) * MSG)
        wait_for(src.at[most], a2a_send_sem.at[n])

    all_to_all(0, sent_slots, got_slots)

    wide[:, PAD - LANES : PAD] = jnp.zeros((WIDTH, LANES), BF16)
    wide[:, 2 * PAD - LANES :] = jnp.zeros((WIDTH, LANES), BF16)
    down[PAD - 64 :, :] = jnp.zeros((64, WIDTH), BF16)
    for copy in weights:
        copy.wait()
    wide[:, :UNITS] = gate_in[...]
    wide[:, PAD : PAD + UNITS] = up_in[...]
    down[:UNITS, :] = down_in[...]

    @pl.loop(0, ZS - 1)
    def _(i):
        zi = far_first(ZS - 2 - i)
        block = tokens.at[y * ZS + zi]
        wait_for(block, zg_recv_sem.at[zi])
        forward_y(zi)

    def send_rows(n, src, dst, chunk):
        @pl.loop(0, ROWS - 1)
        def _(m):
            to = row_peer(m)
            send(
                src.at[pl.ds(pl.multiple_of(to * MINE, MINE), MINE)],
                dst.at[r],
                rs_send_sem.at[n],
                rs_recv_sem.at[n],
                to,
                c,
            ).start()

        dst[r] = src[pl.ds(pl.multiple_of(r * MINE, MINE), MINE), :]

    def sum_rows(n, dst):
        wait_for(dst.at[pl.ds(0, ROWS - 1)], rs_recv_sem.at[n])
        total = dst[0].astype(F32)
        for i in range(1, ROWS):
            total = total + dst[i].astype(F32)
        return total

    def gather_rows(n, buf, rows):
        mine = pl.ds(pl.multiple_of(r * MINE, MINE), MINE)
        buf[mine, :] = rows

        @pl.loop(0, ROWS - 1)
        def _(m):
            send(
                buf.at[mine], buf.at[mine], ag_send_sem.at[n], ag_recv_sem.at[n], row_peer(m), c
            ).start()

    def gather_rows_wait(n, buf):
        wait_for(buf.at[pl.ds(0, (ROWS - 1) * MINE)], ag_recv_sem.at[n])

    def project(n):
        @pl.loop(0, 2 * PAD // TILE)
        def _(i):
            cols = pl.ds(pl.multiple_of(i * TILE, TILE), TILE)
            part[n, :, cols] = dot(rows_in[...], wide[:, cols]).astype(BF16)

        send_rows(n, part.at[n], part_got.at[n], n)

    def load_teacher(n):
        group = lax.rem(y + Y_OFFSETS[n], YS)
        if n > 0:
            block = tokens.at[pl.ds(group * ZS, ZS)]
            wait_for(block, yf_recv_sem.at[Y_OFFSETS[n]])
        blocks = tokens[pl.ds(group * ZS, ZS)].astype(F32).reshape(ZS, SUB, TOK, LANES)
        for j in range(SUB):
            rows_in[:, j * LANES : (j + 1) * LANES] = (
                blocks[:, j].reshape(CHUNK, LANES).astype(BF16)
            )

    def load_slots(got):
        spread[...] = got[...].astype(F32)
        for j in range(SUB):
            rows_in[:, j * LANES : (j + 1) * LANES] = spread[
                pl.ds(j, SLOTS, stride=SUB), :
            ].astype(BF16)

    def activate(n):
        total = sum_rows(n, part_got.at[n])
        gate, up = total[:, :PAD], total[:, PAD:]
        if n == STUDENT:
            pre[...] = total
        gather_rows(n, hidden.at[n], (gate / (1.0 + jnp.exp(-gate)) * up).astype(BF16))

    def store_slots(value, cols, first):
        for j in range(TILE // LANES):
            spread[pl.ds(first + j, SLOTS, stride=SUB), :] = value[:, j * LANES : (j + 1) * LANES]

    def produce_teacher(n):
        gather_rows_wait(n, hidden.at[n])
        for i in range(WIDTH // TILE):
            value = dot(hidden[n], down[:, i * TILE : (i + 1) * TILE])
            halves = [
                value[:, j * LANES : (j + 1) * LANES].reshape(ZS, TOK, LANES)
                for j in range(TILE // LANES)
            ]
            value = jnp.concatenate(halves, axis=1)
            rows = slice(i * 2 * TOK, (i + 1) * 2 * TOK)
            if n == 0:
                own_sum[:, rows, :] = value
            else:
                y_send[n - 1, :, rows, :] = value.astype(BF16)
        if n > 0:
            o = Y_OFFSETS[n]
            to = lax.rem(y + o, YS) * ZS + z

            @pl.loop(0, ZS)
            def _(i):
                zi = far_first(i)
                send(
                    y_send.at[n - 1, zi],
                    y_got.at[zi, n - 1],
                    yr_send_sem,
                    yr_recv_sem.at[zi],
                    r,
                    to,
                ).start()

    def produce_student():
        gather_rows_wait(STUDENT, hidden.at[STUDENT])
        for i in range(WIDTH // TILE):
            value = dot(hidden[STUDENT], down[:, i * TILE : (i + 1) * TILE])
            store_slots(value, i, i * (TILE // LANES))
        back_send[...] = spread[...].astype(BF16)
        all_to_all(1, back_send, back_got)

    for n in range(YS):
        load_teacher(n)
        project(n)
    activate(0)
    activate(1)
    all_to_all_wait(0, sent_slots, got_slots)
    load_slots(got_slots)
    project(STUDENT)
    activate(2)
    activate(3)
    produce_teacher(0)
    produce_teacher(1)
    activate(STUDENT)
    produce_teacher(2)
    produce_teacher(3)
    produce_student()

    @pl.loop(0, ZS)
    def _(i):
        zi = far_first(i)
        wait_for(y_got.at[zi], yr_recv_sem.at[zi])
        got = y_got[zi].astype(F32)
        total = own_sum[zi] + got[0] + got[1] + got[2]
        z_send[zi] = total.astype(BF16)

        @pl.when(i < ZS - 1)
        def _():
            to = y * ZS + zi
            send(z_send.at[zi], z_got.at[z], zr_send_sem, zr_recv_sem, r, to).start()

        @pl.when(i == ZS - 1)
        def _():
            z_got[zi] = total.astype(BF16)

    wait_for(z_got.at[pl.ds(0, ZS - 1)], zr_recv_sem)
    teacher = z_got[0].astype(F32)
    for i in range(1, ZS):
        teacher = teacher + z_got[i].astype(F32)
    teacher = teacher.astype(BF16).astype(F32)
    teacher_out[...] = from_lane_rows(teacher).astype(BF16)

    all_to_all_wait(1, back_send, back_got)
    student = dot(weighting[...], back_got[...]).astype(BF16).astype(F32)
    loss = (student - teacher).astype(BF16)
    loss_send[...] = dot_first(weighting[...], loss).astype(BF16)
    all_to_all(2, loss_send, loss_got)
    student_out[...] = from_lane_rows(student).astype(BF16)

    all_to_all_wait(2, loss_send, loss_got)
    load_slots(loss_got)

    for i in range(PAD // TILE):
        units = slice(i * TILE, (i + 1) * TILE)
        hid_part[:, units] = dot_last(rows_in[...], down[units, :]).astype(BF16)
    send_rows(YS + 1, hid_part, hid_got, 0)
    pre_gate, pre_up = pre[:, :PAD], pre[:, PAD:]
    logistic = 1.0 / (1.0 + jnp.exp(-pre_gate))
    slope = logistic * (1.0 + pre_gate * (1.0 - logistic))
    hidden_grad = sum_rows(YS + 1, hid_got)
    gate_grad = hidden_grad * pre_up * slope
    up_grad = hidden_grad * (pre_gate * logistic)
    both = jnp.concatenate([gate_grad, up_grad], axis=1).astype(BF16)
    gather_rows(YS + 1, grads, both)
    gather_rows_wait(YS + 1, grads)
    for i in range(WIDTH // TILE):
        value = dot_last(grads[...], wide[i * TILE : (i + 1) * TILE, :])
        store_slots(value, i, i * (TILE // LANES))
    last_send[...] = spread[...].astype(BF16)
    all_to_all(3, last_send, last_got)
    all_to_all_wait(3, last_send, last_got)
    grad = dot(placing[...], last_got[...])
    input_grad[...] = from_lane_rows(grad).astype(BF16)

    wait_for(tokens.at[pl.ds(0, ZS - 1)], zg_send_sem)
    wait_for(tokens.at[pl.ds(0, 3 * ZS)], yf_send_sem)
    for n, src in enumerate((sent_slots, back_send, loss_send, last_send)):
        all_to_all_done(n, src)
    for n in range(YS + 1):
        wait_for(part.at[n, pl.ds(0, (ROWS - 1) * MINE)], rs_send_sem.at[n])
        wait_for(hidden.at[n, pl.ds(0, (ROWS - 1) * MINE)], ag_send_sem.at[n])
    wait_for(hid_part.at[pl.ds(0, (ROWS - 1) * MINE)], rs_send_sem.at[YS + 1])
    wait_for(grads.at[pl.ds(0, (ROWS - 1) * MINE)], ag_send_sem.at[YS + 1])
    wait_for(y_send, yr_send_sem)
    wait_for(z_send.at[pl.ds(0, ZS - 1)], zr_send_sem)


def shards(*operands):
    vmem = pl.BlockSpec(memory_space=pltpu.VMEM)
    hbm = pl.BlockSpec(memory_space=pl.ANY)
    out = jax.ShapeDtypeStruct((TOK, WIDTH), BF16)
    sems = pltpu.SemaphoreType.DMA
    return pl.pallas_call(
        kernel,
        out_shape=(out, out, out),
        in_specs=[vmem, vmem, hbm, hbm, hbm, vmem, vmem, vmem],
        out_specs=(vmem, vmem, vmem),
        scratch_shapes=[
            pltpu.VMEM((WIDTH, UNITS), BF16),
            pltpu.VMEM((WIDTH, UNITS), BF16),
            pltpu.VMEM((UNITS, WIDTH), BF16),
            sems((3,)),
            pltpu.VMEM((WIDTH, 2 * PAD), BF16),
            pltpu.VMEM((PAD, WIDTH), BF16),
            pltpu.VMEM((COLS, BLOCK, LANES), BF16),
            pltpu.VMEM((BLOCK, SLOT_ROWS), BF16),
            pltpu.VMEM((BLOCK, SLOT_ROWS), BF16),
            pltpu.VMEM((SLOT_ROWS, LANES), BF16),
            pltpu.VMEM((SLOT_ROWS, LANES), BF16),
            pltpu.VMEM((SLOT_ROWS, LANES), F32),
            pltpu.VMEM((CHUNK, WIDTH), BF16),
            pltpu.VMEM((YS + 1, CHUNK, 2 * PAD), BF16),
            pltpu.VMEM((YS + 1, ROWS, MINE, 2 * PAD), BF16),
            pltpu.VMEM((YS + 1, CHUNK, PAD), BF16),
            pltpu.VMEM((MINE, 2 * PAD), F32),
            pltpu.VMEM((ZS, BLOCK, LANES), F32),
            pltpu.VMEM((YS - 1, ZS, BLOCK, LANES), BF16),
            pltpu.VMEM((ZS, YS - 1, BLOCK, LANES), BF16),
            pltpu.VMEM((ZS, BLOCK, LANES), BF16),
            pltpu.VMEM((ZS, BLOCK, LANES), BF16),
            pltpu.VMEM((SLOT_ROWS, LANES), BF16),
            pltpu.VMEM((SLOT_ROWS, LANES), BF16),
            pltpu.VMEM((SLOT_ROWS, LANES), BF16),
            pltpu.VMEM((SLOT_ROWS, LANES), BF16),
            pltpu.VMEM((CHUNK, PAD), BF16),
            pltpu.VMEM((ROWS, MINE, PAD), BF16),
            pltpu.VMEM((CHUNK, 2 * PAD), BF16),
            pltpu.VMEM((SLOT_ROWS, LANES), BF16),
            pltpu.VMEM((SLOT_ROWS, LANES), BF16),
            sems,
            sems((ZS,)),
            sems,
            sems((YS,)),
            sems((4,)),
            sems((4,)),
            sems((YS + 2,)),
            sems((YS + 2,)),
            sems((YS + 2,)),
            sems((YS + 2,)),
            sems,
            sems((ZS,)),
            sems,
            sems,
            pltpu.SemaphoreType.REGULAR,
        ],
        compiler_params=pltpu.CompilerParams(
            collective_id=0, has_side_effects=True, vmem_limit_bytes=48 * 2**20
        ),
    )(*operands)


def solution(mesh):
    return jax.shard_map(
        shards,
        mesh=mesh,
        in_specs=(
            P("col", "row"),
            P("col", "row"),
            P("row", "col"),
            P("row", "col"),
            P("col", "row"),
            P("col", None),
            P("col", None),
            P("col", None),
        ),
        out_specs=(P("col", "row"), P("col", "row"), P("col", "row")),
        check_vma=False,
    )
```

```python
import functools

import jax
import jax.numpy as jnp
from jax import lax
from jax.experimental import pallas as pl
from jax.experimental.pallas import tpu as pltpu
from jax.sharding import PartitionSpec as P

MESH = pl.DeviceIdType.MESH
F32 = jnp.float32
BF16 = jnp.bfloat16

ROWS = 8
YS, ZS = 4, 16
COLS = YS * ZS
TOK = 8
WIDTH = 1024
LANES = 128
SUB = WIDTH // LANES
UNITS = 462
PAD = 512
CAP = 2
TOPK = 6
SLOTS = COLS * CAP
CHUNK = ZS * TOK
MINE = CHUNK // ROWS
BLOCK = TOK * SUB
MSG = CAP * SUB
SLOT_ROWS = COLS * MSG
STUDENT = YS
Y_OFFSETS = (0, 1, 3, 2)
TILE = 256


def dot(a, b):
    return jnp.dot(a, b, preferred_element_type=F32)


def to_lane_rows(rows):
    return jnp.concatenate([rows[:, j * LANES : (j + 1) * LANES] for j in range(SUB)], axis=0)


def from_lane_rows(block):
    return jnp.concatenate([block[j * TOK : (j + 1) * TOK, :] for j in range(SUB)], axis=1)


def kernel(
    teacher_hbm,
    student_hbm,
    gate_hbm,
    up_hbm,
    down_hbm,
    ids_hbm,
    slots_hbm,
    routes_hbm,
    teacher_out,
    student_out,
    input_grad,
    teacher_ref,
    student_ref,
    gate_in,
    up_in,
    down_in,
    ids_ref,
    slots_ref,
    routes_ref,
    input_sem,
    wide,
    wide_t,
    down,
    down_t,
    tokens,
    placing,
    placing_t,
    weighting,
    weighting_t,
    sent_slots,
    got_slots,
    spread,
    rows_in,
    part,
    part_got,
    hidden,
    pre,
    own_sum,
    y_send,
    y_got,
    z_send,
    z_got,
    back_send,
    back_got,
    loss_send,
    loss_got,
    hid_part,
    hid_got,
    grads,
    last_send,
    last_got,
    zg_send_sem,
    zg_recv_sem,
    yf_send_sem,
    yf_recv_sem,
    a2a_send_sem,
    a2a_recv_sem,
    rs_send_sem,
    rs_recv_sem,
    ag_send_sem,
    ag_recv_sem,
    yr_send_sem,
    yr_recv_sem,
    zr_send_sem,
    zr_recv_sem,
    ready_sem,
):
    r = lax.axis_index("row")
    c = lax.axis_index("col")
    x, core = r // 2, lax.rem(r, 2)
    y, z = c // ZS, lax.rem(c, ZS)

    def row_peer(m):
        return lax.rem(x + 1 + m // 2, 4) * 2 + lax.rem(core + 1 + lax.rem(m, 2), 2)

    def far_first(i):
        distance = ZS // 2 - (i + 1) // 2
        return lax.rem(z + distance * (1 - 2 * lax.rem(i + 1, 2)) + ZS, ZS)

    def col_peer(m):
        return lax.rem(y + 1 + lax.rem(m, YS), YS) * ZS + far_first(m // YS)

    def send(src, dst, send_sem, recv_sem, row, col):
        return pltpu.make_async_remote_copy(
            src_ref=src,
            dst_ref=dst,
            send_sem=send_sem,
            recv_sem=recv_sem,
            device_id=(row, col),
            device_id_type=MESH,
        )

    def wait_for(view, sem):
        pltpu.make_async_copy(view, view, sem).wait()

    owed, left = {}, []

    def owe(name, arrive, leave):
        owed[name] = lambda: wait_for(*arrive)
        left.append(lambda: wait_for(*leave))

    def take(*name):
        owed.pop(name)()

    inputs = [
        pltpu.make_async_copy(a, b, input_sem.at[i])
        for i, (a, b) in enumerate(
            (
                (teacher_hbm, teacher_ref),
                (student_hbm, student_ref),
                (ids_hbm, ids_ref),
                (slots_hbm, slots_ref),
                (routes_hbm, routes_ref),
                (gate_hbm, gate_in),
                (up_hbm, up_in),
                (down_hbm, down_in),
            )
        )
    ]
    for copy in inputs:
        copy.start()
    barrier = pltpu.get_barrier_semaphore()

    @pl.loop(0, ZS - 1)
    def _(i):
        to = y * ZS + far_first(i)
        pl.semaphore_signal(barrier, inc=1, device_id=(r, to), device_id_type=MESH)

    for o in range(1, YS):
        to = lax.rem(y + o, YS) * ZS + z
        pl.semaphore_signal(barrier, inc=1, device_id=(r, to), device_id_type=MESH)

    @pl.loop(0, ROWS - 1)
    def _(m):
        pl.semaphore_signal(barrier, inc=1, device_id=(row_peer(m), c), device_id_type=MESH)

    for copy in inputs[:5]:
        copy.wait()
    tokens[c] = to_lane_rows(teacher_ref[...].astype(F32)).astype(BF16)

    for ref, first in ((wide_t, 0), (wide_t, PAD), (down, 0)):
        ref[first + PAD - 64 : first + PAD, :] = jnp.zeros((64, WIDTH), BF16)
    for copy in inputs[5:]:
        copy.wait()
    wide_t[:UNITS, :] = gate_in[...]
    wide_t[PAD : PAD + UNITS, :] = up_in[...]
    down[:UNITS, :] = down_in[...]

    @pl.loop(0, 2 * PAD // TILE)
    def _(i):
        units = pl.ds(pl.multiple_of(i * TILE, TILE), TILE)
        for k in range(WIDTH // TILE):
            wide[k * TILE : (k + 1) * TILE, units] = wide_t[units, k * TILE : (k + 1) * TILE].T

    targets = (ids_ref[...] * CAP + slots_ref[...]).astype(F32)
    choices = jnp.concatenate([targets, routes_ref[...].astype(F32)], axis=1)
    choices = jnp.concatenate([choices, jnp.zeros((TOK, LANES - 2 * TOPK), F32)], axis=1)
    choices = jnp.concatenate([choices] * SUB, axis=0)
    flipped = choices.T

    def match(slot_of, targets, routes, place_ref, weigh_ref, at):
        place = jnp.zeros(slot_of.shape, F32)
        weigh = jnp.zeros(slot_of.shape, F32)
        for k in range(TOPK):
            hit = slot_of == targets(k)
            place = jnp.where(hit, 1.0, place)
            weigh = jnp.where(hit, routes(k), weigh)
        place_ref[at] = place.astype(BF16)
        weigh_ref[at] = weigh.astype(BF16)

    for i in range(SLOT_ROWS // LANES):
        shape = (BLOCK, LANES)
        row = lax.broadcasted_iota(jnp.int32, shape, 0)
        col = lax.broadcasted_iota(jnp.int32, shape, 1) + i * LANES
        slot_of = jnp.where((col & (SUB - 1)) == (row >> 3), col >> 3, -1).astype(F32)
        match(
            slot_of,
            lambda k: choices[:, k : k + 1],
            lambda k: choices[:, TOPK + k : TOPK + k + 1],
            placing,
            weighting,
            (slice(None), slice(i * LANES, (i + 1) * LANES)),
        )
        shape = (LANES, BLOCK)
        row = lax.broadcasted_iota(jnp.int32, shape, 0) + i * LANES
        col = lax.broadcasted_iota(jnp.int32, shape, 1)
        slot_of = jnp.where((row & (SUB - 1)) == (col >> 3), row >> 3, -1).astype(F32)
        match(
            slot_of,
            lambda k: flipped[k : k + 1, :],
            lambda k: flipped[TOPK + k : TOPK + k + 1, :],
            placing_t,
            weighting_t,
            (slice(i * LANES, (i + 1) * LANES), slice(None)),
        )
    student_rows = to_lane_rows(student_ref[...].astype(F32)).astype(BF16)
    sent_slots[...] = dot(placing_t[...], student_rows).astype(BF16)

    pl.semaphore_wait(barrier, ZS + YS - 2 + ROWS - 1)

    def gather_z(i):
        to = y * ZS + lax.rem(z + i, ZS)
        return send(tokens.at[c], tokens.at[c], zg_send_sem, zg_recv_sem.at[z], r, to)

    for o in [1, 15, 2, 14, 3, 13, 4, 12, 5, 11, 6, 10, 7, 9, 8]:
        gather_z(o).start()

    def forward_y(zi):
        block = tokens.at[y * ZS + zi]
        for o in (2, 1, 3):
            to = lax.rem(y + o, YS) * ZS + z
            send(block, block, yf_send_sem, yf_recv_sem.at[YS - o], r, to).start()

    left.append(lambda: wait_for(tokens.at[pl.ds(0, ZS - 1)], zg_send_sem))
    left.append(lambda: wait_for(tokens.at[pl.ds(0, 3 * ZS)], yf_send_sem))
    forward_y(z)

    for o in range(1, YS):
        to = lax.rem(y + o, YS) * ZS + z
        pl.semaphore_signal(ready_sem, inc=1, device_id=(r, to), device_id_type=MESH)
    pl.semaphore_wait(ready_sem, YS - 1)

    def all_to_all(n, src, dst):
        @pl.loop(0, COLS - 1)
        def _(m):
            to = col_peer(m)
            send(
                src.at[pl.ds(pl.multiple_of(to * MSG, MSG), MSG)],
                dst.at[pl.ds(pl.multiple_of(c * MSG, MSG), MSG)],
                a2a_send_sem.at[n],
                a2a_recv_sem.at[n],
                r,
                to,
            ).start()

        own = pl.ds(pl.multiple_of(c * MSG, MSG), MSG)
        dst[own, :] = src[own, :]
        most = pl.ds(0, (COLS - 1) * MSG)
        owe(("slots", n), (dst.at[most], a2a_recv_sem.at[n]), (src.at[most], a2a_send_sem.at[n]))

    for o in [1, 15, 2, 14, 3, 13, 4, 12, 5, 11, 6, 10, 7, 9, 8]:
        zi = lax.rem(z + o, ZS)
        block = tokens.at[y * ZS + zi]
        wait_for(block, zg_recv_sem.at[zi])
        forward_y(zi)

    all_to_all(0, sent_slots, got_slots)

    for n in range(1, YS):
        group = lax.rem(y + Y_OFFSETS[n], YS)
        block = tokens.at[pl.ds(group * ZS, ZS)]
        owed["tokens", n] = functools.partial(wait_for, block, yf_recv_sem.at[Y_OFFSETS[n]])


    def send_rows(n, src, dst):
        @pl.loop(0, ROWS - 1)
        def _(m):
            to = row_peer(m)
            send(
                src.at[pl.ds(pl.multiple_of(to * MINE, MINE), MINE)],
                dst.at[r],
                rs_send_sem.at[n],
                rs_recv_sem.at[n],
                to,
                c,
            ).start()

        dst[r] = src[pl.ds(pl.multiple_of(r * MINE, MINE), MINE), :]
        leave = src.at[pl.ds(0, (ROWS - 1) * MINE)]
        owe(
            ("sum", n),
            (dst.at[pl.ds(0, ROWS - 1)], rs_recv_sem.at[n]),
            (leave, rs_send_sem.at[n]),
        )

    def sum_rows(n, dst):
        take("sum", n)
        total = dst[0].astype(F32)
        for i in range(1, ROWS):
            total = total + dst[i].astype(F32)
        return total

    def gather_rows(n, buf, rows):
        mine = pl.ds(pl.multiple_of(r * MINE, MINE), MINE)
        buf[mine, :] = rows

        @pl.loop(0, ROWS - 1)
        def _(m):
            send(
                buf.at[mine], buf.at[mine], ag_send_sem.at[n], ag_recv_sem.at[n], row_peer(m), c
            ).start()

        most = buf.at[pl.ds(0, (ROWS - 1) * MINE)]
        owe(("gather", n), (most, ag_recv_sem.at[n]), (most, ag_send_sem.at[n]))

    def project(n):
        @pl.loop(0, 2 * PAD // TILE)
        def _(i):
            cols = pl.ds(pl.multiple_of(i * TILE, TILE), TILE)
            part[n, :, cols] = dot(rows_in[...], wide[:, cols]).astype(BF16)

        send_rows(n, part.at[n], part_got.at[n])

    def load_teacher(n):
        group = lax.rem(y + Y_OFFSETS[n], YS)
        if n > 0:
            take("tokens", n)
        blocks = tokens[pl.ds(group * ZS, ZS)].astype(F32).reshape(ZS, SUB, TOK, LANES)
        for j in range(SUB):
            rows_in[:, j * LANES : (j + 1) * LANES] = (
                blocks[:, j].reshape(CHUNK, LANES).astype(BF16)
            )

    def load_slots(got):
        spread[...] = got[...].astype(F32)
        for j in range(SUB):
            rows_in[:, j * LANES : (j + 1) * LANES] = spread[
                pl.ds(j, SLOTS, stride=SUB), :
            ].astype(BF16)

    def activate(n):
        total = sum_rows(n, part_got.at[n])
        gate, up = total[:, :PAD], total[:, PAD:]
        if n == STUDENT:
            pre[...] = total
        gather_rows(n, hidden.at[n], (gate / (1.0 + jnp.exp(-gate)) * up).astype(BF16))

    def store_slots(value, cols, first):
        for j in range(TILE // LANES):
            spread[pl.ds(first + j, SLOTS, stride=SUB), :] = value[:, j * LANES : (j + 1) * LANES]

    def produce_teacher(n):
        take("gather", n)
        for i in range(WIDTH // TILE):
            value = dot(hidden[n], down[:, i * TILE : (i + 1) * TILE])
            halves = [
                value[:, j * LANES : (j + 1) * LANES].reshape(ZS, TOK, LANES)
                for j in range(TILE // LANES)
            ]
            value = jnp.concatenate(halves, axis=1)
            rows = slice(i * 2 * TOK, (i + 1) * 2 * TOK)
            if n == 0:
                own_sum[:, rows, :] = value
            else:
                y_send[n - 1, :, rows, :] = value.astype(BF16)
        if n > 0:
            o = Y_OFFSETS[n]
            to = lax.rem(y + o, YS) * ZS + z
            left.append(lambda: wait_for(y_send.at[n - 1], yr_send_sem))

            @pl.loop(0, ZS)
            def _(i):
                zi = far_first(i)
                send(
                    y_send.at[n - 1, zi],
                    y_got.at[zi, n - 1],
                    yr_send_sem,
                    yr_recv_sem.at[zi],
                    r,
                    to,
                ).start()

    def produce_student():
        take("gather", STUDENT)
        for i in range(WIDTH // TILE):
            value = dot(hidden[STUDENT], down[:, i * TILE : (i + 1) * TILE])
            store_slots(value, i, i * (TILE // LANES))
        back_send[...] = spread[...].astype(BF16)
        all_to_all(1, back_send, back_got)

    for n in range(YS):
        load_teacher(n)
        project(n)
    activate(0)
    activate(1)
    take("slots", 0)
    load_slots(got_slots)
    project(STUDENT)
    activate(2)
    activate(3)
    produce_teacher(1)
    produce_teacher(2)
    activate(STUDENT)
    produce_teacher(3)
    produce_student()
    produce_teacher(0)

    @pl.loop(0, ZS)
    def _(i):
        zi = far_first(i)
        wait_for(y_got.at[zi], yr_recv_sem.at[zi])
        got = y_got[zi].astype(F32)
        total = own_sum[zi] + got[0] + got[1] + got[2]
        z_send[zi] = total.astype(BF16)

        @pl.when(i < ZS - 1)
        def _():
            to = y * ZS + zi
            send(z_send.at[zi], z_got.at[z], zr_send_sem, zr_recv_sem, r, to).start()

        @pl.when(i == ZS - 1)
        def _():
            z_got[zi] = total.astype(BF16)

    left.append(lambda: wait_for(z_send.at[pl.ds(0, ZS - 1)], zr_send_sem))

    @pl.loop(0, PAD // TILE)
    def _(i):
        units = pl.ds(pl.multiple_of(i * TILE, TILE), TILE)
        for k in range(WIDTH // TILE):
            down_t[k * TILE : (k + 1) * TILE, units] = down[units, k * TILE : (k + 1) * TILE].T

    wait_for(z_got.at[pl.ds(0, ZS - 1)], zr_recv_sem)
    teacher = z_got[0].astype(F32)
    for i in range(1, ZS):
        teacher = teacher + z_got[i].astype(F32)
    teacher = teacher.astype(BF16).astype(F32)
    teacher_out[...] = from_lane_rows(teacher).astype(BF16)

    take("slots", 1)
    student = dot(weighting[...], back_got[...]).astype(BF16).astype(F32)
    loss = (student - teacher).astype(BF16)
    loss_send[...] = dot(weighting_t[...], loss).astype(BF16)
    all_to_all(2, loss_send, loss_got)
    student_out[...] = from_lane_rows(student).astype(BF16)

    take("slots", 2)
    load_slots(loss_got)

    for i in range(PAD // TILE):
        units = slice(i * TILE, (i + 1) * TILE)
        hid_part[:, units] = dot(rows_in[...], down_t[:, units]).astype(BF16)
    send_rows(YS + 1, hid_part, hid_got)
    pre_gate, pre_up = pre[:, :PAD], pre[:, PAD:]
    logistic = 1.0 / (1.0 + jnp.exp(-pre_gate))
    slope = logistic * (1.0 + pre_gate * (1.0 - logistic))
    hidden_grad = sum_rows(YS + 1, hid_got)
    gate_grad = hidden_grad * pre_up * slope
    up_grad = hidden_grad * (pre_gate * logistic)
    both = jnp.concatenate([gate_grad, up_grad], axis=1).astype(BF16)
    gather_rows(YS + 1, grads, both)
    take("gather", YS + 1)
    for i in range(WIDTH // TILE):
        value = dot(grads[...], wide_t[:, i * TILE : (i + 1) * TILE])
        store_slots(value, i, i * (TILE // LANES))
    last_send[...] = spread[...].astype(BF16)
    all_to_all(3, last_send, last_got)
    take("slots", 3)
    grad = dot(placing[...], last_got[...])
    input_grad[...] = from_lane_rows(grad).astype(BF16)

    for wait in left:
        wait()


def shards(teacher, student, gate, up, down, ids, slots, routes):
    vmem = pl.BlockSpec(memory_space=pltpu.VMEM)
    hbm = pl.BlockSpec(memory_space=pltpu.HBM)
    out = jax.ShapeDtypeStruct((TOK, WIDTH), BF16)
    sems = pltpu.SemaphoreType.DMA
    return pl.pallas_call(
        kernel,
        out_shape=(out, out, out),
        in_specs=[hbm] * 8,
        out_specs=(vmem, vmem, vmem),
        scratch_shapes=[
            pltpu.VMEM((TOK, WIDTH), BF16),
            pltpu.VMEM((TOK, WIDTH), BF16),
            pltpu.VMEM((UNITS, WIDTH), BF16),
            pltpu.VMEM((UNITS, WIDTH), BF16),
            pltpu.VMEM((UNITS, WIDTH), BF16),
            pltpu.VMEM((TOK, TOPK), jnp.int32),
            pltpu.VMEM((TOK, TOPK), jnp.int32),
            pltpu.VMEM((TOK, TOPK), BF16),
            sems((8,)),
            pltpu.VMEM((WIDTH, 2 * PAD), BF16),
            pltpu.VMEM((2 * PAD, WIDTH), BF16),
            pltpu.VMEM((PAD, WIDTH), BF16),
            pltpu.VMEM((WIDTH, PAD), BF16),
            pltpu.VMEM((COLS, BLOCK, LANES), BF16),
            pltpu.VMEM((BLOCK, SLOT_ROWS), BF16),
            pltpu.VMEM((SLOT_ROWS, BLOCK), BF16),
            pltpu.VMEM((BLOCK, SLOT_ROWS), BF16),
            pltpu.VMEM((SLOT_ROWS, BLOCK), BF16),
            pltpu.VMEM((SLOT_ROWS, LANES), BF16),
            pltpu.VMEM((SLOT_ROWS, LANES), BF16),
            pltpu.VMEM((SLOT_ROWS, LANES), F32),
            pltpu.VMEM((CHUNK, WIDTH), BF16),
            pltpu.VMEM((YS + 1, CHUNK, 2 * PAD), BF16),
            pltpu.VMEM((YS + 1, ROWS, MINE, 2 * PAD), BF16),
            pltpu.VMEM((YS + 1, CHUNK, PAD), BF16),
            pltpu.VMEM((MINE, 2 * PAD), F32),
            pltpu.VMEM((ZS, BLOCK, LANES), F32),
            pltpu.VMEM((YS - 1, ZS, BLOCK, LANES), BF16),
            pltpu.VMEM((ZS, YS - 1, BLOCK, LANES), BF16),
            pltpu.VMEM((ZS, BLOCK, LANES), BF16),
            pltpu.VMEM((ZS, BLOCK, LANES), BF16),
            pltpu.VMEM((SLOT_ROWS, LANES), BF16),
            pltpu.VMEM((SLOT_ROWS, LANES), BF16),
            pltpu.VMEM((SLOT_ROWS, LANES), BF16),
            pltpu.VMEM((SLOT_ROWS, LANES), BF16),
            pltpu.VMEM((CHUNK, PAD), BF16),
            pltpu.VMEM((ROWS, MINE, PAD), BF16),
            pltpu.VMEM((CHUNK, 2 * PAD), BF16),
            pltpu.VMEM((SLOT_ROWS, LANES), BF16),
            pltpu.VMEM((SLOT_ROWS, LANES), BF16),
            sems,
            sems((ZS,)),
            sems,
            sems((YS,)),
            sems((4,)),
            sems((4,)),
            sems((YS + 2,)),
            sems((YS + 2,)),
            sems((YS + 2,)),
            sems((YS + 2,)),
            sems,
            sems((ZS,)),
            sems,
            sems,
            pltpu.SemaphoreType.REGULAR,
        ],
        compiler_params=pltpu.CompilerParams(
            collective_id=0, has_side_effects=True, vmem_limit_bytes=64 * 2**20
        ),
    )(teacher, student, gate.T, up.T, down, ids, slots, routes)


def solution(mesh):
    return jax.shard_map(
        shards,
        mesh=mesh,
        in_specs=(
            P("col", "row"),
            P("col", "row"),
            P("row", "col"),
            P("row", "col"),
            P("col", "row"),
            P("col", None),
            P("col", None),
            P("col", None),
        ),
        out_specs=(P("col", "row"), P("col", "row"), P("col", "row")),
        check_vma=False,
    )
```

```python
import functools

import jax
import jax.numpy as jnp
from jax import lax
from jax.experimental import pallas as pl
from jax.experimental.pallas import tpu as pltpu
from jax.sharding import PartitionSpec as P

MESH = pl.DeviceIdType.MESH
F32 = jnp.float32
BF16 = jnp.bfloat16

ROWS = 8
XS = 4
YS, ZS = 4, 16
COLS = YS * ZS
TOK = 8
WIDTH = 1024
LANES = 128
SUB = WIDTH // LANES
UNITS = 462
PAD = 512
CAP = 2
TOPK = 6
SLOTS = COLS * CAP
CHUNK = ZS * TOK
MINE = CHUNK // ROWS
BLOCK = TOK * SUB
MSG = CAP * SUB
SLOT_ROWS = COLS * MSG
STUDENT = YS
Y_OFFSETS = (0, 1, 3, 2)
TILE = 256


def dot(a, b):
    return jnp.dot(a, b, preferred_element_type=F32)


def to_lane_rows(rows):
    return jnp.concatenate([rows[:, j * LANES : (j + 1) * LANES] for j in range(SUB)], axis=0)


def from_lane_rows(block):
    return jnp.concatenate([block[j * TOK : (j + 1) * TOK, :] for j in range(SUB)], axis=1)


def kernel(
    teacher_hbm,
    student_hbm,
    gate_hbm,
    up_hbm,
    down_hbm,
    ids_hbm,
    slots_hbm,
    routes_hbm,
    teacher_out,
    student_out,
    input_grad,
    teacher_ref,
    student_ref,
    gate_in,
    up_in,
    down_in,
    ids_ref,
    slots_ref,
    routes_ref,
    input_sem,
    wide,
    wide_t,
    down,
    down_t,
    tokens,
    placing,
    placing_t,
    weighting,
    weighting_t,
    sent_slots,
    got_slots,
    spread,
    rows_in,
    part,
    pair,
    pair_got,
    part_got,
    hidden,
    pre,
    own_sum,
    y_send,
    y_got,
    z_send,
    z_got,
    back_send,
    back_got,
    loss_send,
    loss_got,
    hid_part,
    hid_got,
    grads,
    last_send,
    last_got,
    zg_send_sem,
    zg_recv_sem,
    yf_send_sem,
    yf_recv_sem,
    a2a_send_sem,
    a2a_recv_sem,
    pair_send_sem,
    pair_recv_sem,
    rs_send_sem,
    rs_recv_sem,
    ag_send_sem,
    ag_recv_sem,
    yr_send_sem,
    yr_recv_sem,
    zr_send_sem,
    zr_recv_sem,
    ready_sem,
):
    r = lax.axis_index("row")
    c = lax.axis_index("col")
    x, core = r // 2, lax.rem(r, 2)
    y, z = c // ZS, lax.rem(c, ZS)

    def row_peer(m):
        return lax.rem(x + 1 + m // 2, 4) * 2 + lax.rem(core + 1 + lax.rem(m, 2), 2)

    def far_first(i):
        distance = ZS // 2 - (i + 1) // 2
        return lax.rem(z + distance * (1 - 2 * lax.rem(i + 1, 2)) + ZS, ZS)

    def col_peer(m):
        return lax.rem(y + 1 + lax.rem(m, YS), YS) * ZS + far_first(m // YS)

    def send(src, dst, send_sem, recv_sem, row, col):
        return pltpu.make_async_remote_copy(
            src_ref=src,
            dst_ref=dst,
            send_sem=send_sem,
            recv_sem=recv_sem,
            device_id=(row, col),
            device_id_type=MESH,
        )

    def wait_for(view, sem):
        pltpu.make_async_copy(view, view, sem).wait()

    owed, left = {}, []

    def owe(name, arrive, leave):
        owed[name] = lambda: wait_for(*arrive)
        left.append(lambda: wait_for(*leave))

    def take(*name):
        owed.pop(name)()

    inputs = [
        pltpu.make_async_copy(a, b, input_sem.at[i])
        for i, (a, b) in enumerate(
            (
                (teacher_hbm, teacher_ref),
                (student_hbm, student_ref),
                (ids_hbm, ids_ref),
                (slots_hbm, slots_ref),
                (routes_hbm, routes_ref),
                (gate_hbm, gate_in),
                (up_hbm, up_in),
                (down_hbm, down_in),
            )
        )
    ]
    for copy in inputs:
        copy.start()
    barrier = pltpu.get_barrier_semaphore()

    @pl.loop(0, ZS - 1)
    def _(i):
        to = y * ZS + far_first(i)
        pl.semaphore_signal(barrier, inc=1, device_id=(r, to), device_id_type=MESH)

    for o in range(1, YS):
        to = lax.rem(y + o, YS) * ZS + z
        pl.semaphore_signal(barrier, inc=1, device_id=(r, to), device_id_type=MESH)

    @pl.loop(0, ROWS - 1)
    def _(m):
        pl.semaphore_signal(barrier, inc=1, device_id=(row_peer(m), c), device_id_type=MESH)

    for copy in inputs[:5]:
        copy.wait()
    tokens[c] = to_lane_rows(teacher_ref[...].astype(F32)).astype(BF16)

    for ref, first in ((wide_t, 0), (wide_t, PAD), (down, 0)):
        ref[first + PAD - 64 : first + PAD, :] = jnp.zeros((64, WIDTH), BF16)
    for copy in inputs[5:]:
        copy.wait()
    wide_t[:UNITS, :] = gate_in[...]
    wide_t[PAD : PAD + UNITS, :] = up_in[...]
    down[:UNITS, :] = down_in[...]

    @pl.loop(0, 2 * PAD // TILE)
    def _(i):
        units = pl.ds(pl.multiple_of(i * TILE, TILE), TILE)
        for k in range(WIDTH // TILE):
            wide[k * TILE : (k + 1) * TILE, units] = wide_t[units, k * TILE : (k + 1) * TILE].T

    targets = (ids_ref[...] * CAP + slots_ref[...]).astype(F32)
    choices = jnp.concatenate([targets, routes_ref[...].astype(F32)], axis=1)
    choices = jnp.concatenate([choices, jnp.zeros((TOK, LANES - 2 * TOPK), F32)], axis=1)
    choices = jnp.concatenate([choices] * SUB, axis=0)
    flipped = choices.T

    def match(slot_of, targets, routes, place_ref, weigh_ref, at):
        place = jnp.zeros(slot_of.shape, F32)
        weigh = jnp.zeros(slot_of.shape, F32)
        for k in range(TOPK):
            hit = slot_of == targets(k)
            place = jnp.where(hit, 1.0, place)
            weigh = jnp.where(hit, routes(k), weigh)
        place_ref[at] = place.astype(BF16)
        weigh_ref[at] = weigh.astype(BF16)

    for i in range(SLOT_ROWS // LANES):
        shape = (BLOCK, LANES)
        row = lax.broadcasted_iota(jnp.int32, shape, 0)
        col = lax.broadcasted_iota(jnp.int32, shape, 1) + i * LANES
        slot_of = jnp.where((col & (SUB - 1)) == (row >> 3), col >> 3, -1).astype(F32)
        match(
            slot_of,
            lambda k: choices[:, k : k + 1],
            lambda k: choices[:, TOPK + k : TOPK + k + 1],
            placing,
            weighting,
            (slice(None), slice(i * LANES, (i + 1) * LANES)),
        )
        shape = (LANES, BLOCK)
        row = lax.broadcasted_iota(jnp.int32, shape, 0) + i * LANES
        col = lax.broadcasted_iota(jnp.int32, shape, 1)
        slot_of = jnp.where((row & (SUB - 1)) == (col >> 3), row >> 3, -1).astype(F32)
        match(
            slot_of,
            lambda k: flipped[k : k + 1, :],
            lambda k: flipped[TOPK + k : TOPK + k + 1, :],
            placing_t,
            weighting_t,
            (slice(i * LANES, (i + 1) * LANES), slice(None)),
        )
    student_rows = to_lane_rows(student_ref[...].astype(F32)).astype(BF16)
    sent_slots[...] = dot(placing_t[...], student_rows).astype(BF16)

    pl.semaphore_wait(barrier, ZS + YS - 2 + ROWS - 1)

    def gather_z(i):
        to = y * ZS + lax.rem(z + i, ZS)
        return send(tokens.at[c], tokens.at[c], zg_send_sem, zg_recv_sem.at[z], r, to)

    for o in [1, 15, 2, 14, 3, 13, 4, 12, 5, 11, 6, 10, 7, 9, 8]:
        gather_z(o).start()

    def forward_y(zi):
        block = tokens.at[y * ZS + zi]
        for o in (2, 1, 3):
            to = lax.rem(y + o, YS) * ZS + z
            send(block, block, yf_send_sem, yf_recv_sem.at[YS - o], r, to).start()

    left.append(lambda: wait_for(tokens.at[pl.ds(0, ZS - 1)], zg_send_sem))
    left.append(lambda: wait_for(tokens.at[pl.ds(0, 3 * ZS)], yf_send_sem))
    forward_y(z)

    for o in range(1, YS):
        to = lax.rem(y + o, YS) * ZS + z
        pl.semaphore_signal(ready_sem, inc=1, device_id=(r, to), device_id_type=MESH)
    pl.semaphore_wait(ready_sem, YS - 1)

    def all_to_all(n, src, dst):
        @pl.loop(0, COLS - 1)
        def _(m):
            to = col_peer(m)
            send(
                src.at[pl.ds(pl.multiple_of(to * MSG, MSG), MSG)],
                dst.at[pl.ds(pl.multiple_of(c * MSG, MSG), MSG)],
                a2a_send_sem.at[n],
                a2a_recv_sem.at[n],
                r,
                to,
            ).start()

        own = pl.ds(pl.multiple_of(c * MSG, MSG), MSG)
        dst[own, :] = src[own, :]
        most = pl.ds(0, (COLS - 1) * MSG)
        owe(("slots", n), (dst.at[most], a2a_recv_sem.at[n]), (src.at[most], a2a_send_sem.at[n]))

    for o in [1, 15, 2, 14, 3, 13, 4, 12, 5, 11, 6, 10, 7, 9, 8]:
        zi = lax.rem(z + o, ZS)
        block = tokens.at[y * ZS + zi]
        wait_for(block, zg_recv_sem.at[zi])
        forward_y(zi)

    all_to_all(0, sent_slots, got_slots)

    for n in range(1, YS):
        group = lax.rem(y + Y_OFFSETS[n], YS)
        block = tokens.at[pl.ds(group * ZS, ZS)]
        owed["tokens", n] = functools.partial(wait_for, block, yf_recv_sem.at[Y_OFFSETS[n]])


    def send_rows(n, src, dst):
        @pl.loop(0, ROWS - 1)
        def _(m):
            to = row_peer(m)
            send(
                src.at[pl.ds(pl.multiple_of(to * MINE, MINE), MINE)],
                dst.at[r],
                rs_send_sem.at[n],
                rs_recv_sem.at[n],
                to,
                c,
            ).start()

        dst[r] = src[pl.ds(pl.multiple_of(r * MINE, MINE), MINE), :]
        leave = src.at[pl.ds(0, (ROWS - 1) * MINE)]
        owe(
            ("sum", n),
            (dst.at[pl.ds(0, ROWS - 1)], rs_recv_sem.at[n]),
            (leave, rs_send_sem.at[n]),
        )

    def sum_rows(n, dst):
        take("sum", n)
        total = dst[0].astype(F32)
        for i in range(1, dst.shape[0]):
            total = total + dst[i].astype(F32)
        return total

    def gather_rows(n, buf, rows):
        mine = pl.ds(pl.multiple_of(r * MINE, MINE), MINE)
        buf[mine, :] = rows

        @pl.loop(0, ROWS - 1)
        def _(m):
            send(
                buf.at[mine], buf.at[mine], ag_send_sem.at[n], ag_recv_sem.at[n], row_peer(m), c
            ).start()

        most = buf.at[pl.ds(0, (ROWS - 1) * MINE)]
        owe(("gather", n), (most, ag_recv_sem.at[n]), (most, ag_send_sem.at[n]))

    def project(n):
        @pl.loop(0, 2 * PAD // TILE)
        def _(i):
            cols = pl.ds(pl.multiple_of(i * TILE, TILE), TILE)
            value = dot(rows_in[...], wide[:, cols]).reshape(XS, 2, MINE, TILE)
            part[n, :, :, :, cols] = value.astype(BF16)

        other = part.at[n, :, 1 - core]
        got = pair_got.at[n]
        send(other, got, pair_send_sem.at[n], pair_recv_sem.at[n], x * 2 + 1 - core, c).start()
        owe(("pair", n), (got, pair_recv_sem.at[n]), (got, pair_send_sem.at[n]))

    def combine(n):
        take("pair", n)
        pair[n] = (part[n, :, core].astype(F32) + pair_got[n].astype(F32)).astype(BF16)
        for o in (2, 1, 3):
            to = lax.rem(x + o, XS)
            send(
                pair.at[n, to],
                part_got.at[n, x],
                rs_send_sem.at[n],
                rs_recv_sem.at[n],
                to * 2 + core,
                c,
            ).start()
        part_got[n, x] = pair[n, x]
        most = pl.ds(0, XS - 1)
        owe(
            ("sum", n),
            (part_got.at[n, most], rs_recv_sem.at[n]),
            (pair.at[n, most], rs_send_sem.at[n]),
        )

    def load_teacher(n):
        group = lax.rem(y + Y_OFFSETS[n], YS)
        if n > 0:
            take("tokens", n)
        blocks = tokens[pl.ds(group * ZS, ZS)].astype(F32).reshape(ZS, SUB, TOK, LANES)
        for j in range(SUB):
            rows_in[:, j * LANES : (j + 1) * LANES] = (
                blocks[:, j].reshape(CHUNK, LANES).astype(BF16)
            )

    def load_slots(got):
        spread[...] = got[...].astype(F32)
        for j in range(SUB):
            rows_in[:, j * LANES : (j + 1) * LANES] = spread[
                pl.ds(j, SLOTS, stride=SUB), :
            ].astype(BF16)

    def activate(n):
        total = sum_rows(n, part_got.at[n])
        gate, up = total[:, :PAD], total[:, PAD:]
        if n == STUDENT:
            pre[...] = total
        gather_rows(n, hidden.at[n], (gate / (1.0 + jnp.exp(-gate)) * up).astype(BF16))

    def store_slots(value, cols, first):
        for j in range(TILE // LANES):
            spread[pl.ds(first + j, SLOTS, stride=SUB), :] = value[:, j * LANES : (j + 1) * LANES]

    def produce_teacher(n):
        take("gather", n)
        for i in range(WIDTH // TILE):
            value = dot(hidden[n], down[:, i * TILE : (i + 1) * TILE])
            halves = [
                value[:, j * LANES : (j + 1) * LANES].reshape(ZS, TOK, LANES)
                for j in range(TILE // LANES)
            ]
            value = jnp.concatenate(halves, axis=1)
            rows = slice(i * 2 * TOK, (i + 1) * 2 * TOK)
            if n == 0:
                own_sum[:, rows, :] = value
            else:
                y_send[n - 1, :, rows, :] = value.astype(BF16)
        if n > 0:
            o = Y_OFFSETS[n]
            to = lax.rem(y + o, YS) * ZS + z
            left.append(lambda: wait_for(y_send.at[n - 1], yr_send_sem))

            @pl.loop(0, ZS)
            def _(i):
                zi = far_first(i)
                send(
                    y_send.at[n - 1, zi],
                    y_got.at[zi, n - 1],
                    yr_send_sem,
                    yr_recv_sem.at[zi],
                    r,
                    to,
                ).start()

    def produce_student():
        take("gather", STUDENT)
        for i in range(WIDTH // TILE):
            value = dot(hidden[STUDENT], down[:, i * TILE : (i + 1) * TILE])
            store_slots(value, i, i * (TILE // LANES))
        back_send[...] = spread[...].astype(BF16)
        all_to_all(1, back_send, back_got)

    load_teacher(0)
    project(0)
    load_teacher(1)
    project(1)
    combine(0)
    load_teacher(2)
    project(2)
    combine(1)
    load_teacher(3)
    project(3)
    combine(2)
    activate(0)
    combine(3)
    activate(1)
    take("slots", 0)
    load_slots(got_slots)
    project(STUDENT)
    activate(2)
    combine(STUDENT)
    activate(3)
    produce_teacher(1)
    produce_teacher(2)
    activate(STUDENT)
    produce_teacher(3)
    produce_student()
    produce_teacher(0)

    @pl.loop(0, ZS)
    def _(i):
        zi = far_first(i)
        wait_for(y_got.at[zi], yr_recv_sem.at[zi])
        got = y_got[zi].astype(F32)
        total = own_sum[zi] + got[0] + got[1] + got[2]
        z_send[zi] = total.astype(BF16)

        @pl.when(i < ZS - 1)
        def _():
            to = y * ZS + zi
            send(z_send.at[zi], z_got.at[z], zr_send_sem, zr_recv_sem, r, to).start()

        @pl.when(i == ZS - 1)
        def _():
            z_got[zi] = total.astype(BF16)

    left.append(lambda: wait_for(z_send.at[pl.ds(0, ZS - 1)], zr_send_sem))

    @pl.loop(0, PAD // TILE)
    def _(i):
        units = pl.ds(pl.multiple_of(i * TILE, TILE), TILE)
        for k in range(WIDTH // TILE):
            down_t[k * TILE : (k + 1) * TILE, units] = down[units, k * TILE : (k + 1) * TILE].T

    wait_for(z_got.at[pl.ds(0, ZS - 1)], zr_recv_sem)
    teacher = z_got[0].astype(F32)
    for i in range(1, ZS):
        teacher = teacher + z_got[i].astype(F32)
    teacher = teacher.astype(BF16).astype(F32)
    teacher_out[...] = from_lane_rows(teacher).astype(BF16)

    take("slots", 1)
    student = dot(weighting[...], back_got[...]).astype(BF16).astype(F32)
    loss = (student - teacher).astype(BF16)
    loss_send[...] = dot(weighting_t[...], loss).astype(BF16)
    all_to_all(2, loss_send, loss_got)
    student_out[...] = from_lane_rows(student).astype(BF16)

    take("slots", 2)
    load_slots(loss_got)

    for i in range(PAD // TILE):
        units = slice(i * TILE, (i + 1) * TILE)
        hid_part[:, units] = dot(rows_in[...], down_t[:, units]).astype(BF16)
    send_rows(YS + 1, hid_part, hid_got)
    pre_gate, pre_up = pre[:, :PAD], pre[:, PAD:]
    logistic = 1.0 / (1.0 + jnp.exp(-pre_gate))
    slope = logistic * (1.0 + pre_gate * (1.0 - logistic))
    hidden_grad = sum_rows(YS + 1, hid_got)
    gate_grad = hidden_grad * pre_up * slope
    up_grad = hidden_grad * (pre_gate * logistic)
    both = jnp.concatenate([gate_grad, up_grad], axis=1).astype(BF16)
    gather_rows(YS + 1, grads, both)
    take("gather", YS + 1)
    for i in range(WIDTH // TILE):
        value = dot(grads[...], wide_t[:, i * TILE : (i + 1) * TILE])
        store_slots(value, i, i * (TILE // LANES))
    last_send[...] = spread[...].astype(BF16)
    all_to_all(3, last_send, last_got)
    take("slots", 3)
    grad = dot(placing[...], last_got[...])
    input_grad[...] = from_lane_rows(grad).astype(BF16)

    for wait in left:
        wait()


def shards(teacher, student, gate, up, down, ids, slots, routes):
    vmem = pl.BlockSpec(memory_space=pltpu.VMEM)
    hbm = pl.BlockSpec(memory_space=pltpu.HBM)
    out = jax.ShapeDtypeStruct((TOK, WIDTH), BF16)
    sems = pltpu.SemaphoreType.DMA
    return pl.pallas_call(
        kernel,
        out_shape=(out, out, out),
        in_specs=[hbm] * 8,
        out_specs=(vmem, vmem, vmem),
        scratch_shapes=[
            pltpu.VMEM((TOK, WIDTH), BF16),
            pltpu.VMEM((TOK, WIDTH), BF16),
            pltpu.VMEM((UNITS, WIDTH), BF16),
            pltpu.VMEM((UNITS, WIDTH), BF16),
            pltpu.VMEM((UNITS, WIDTH), BF16),
            pltpu.VMEM((TOK, TOPK), jnp.int32),
            pltpu.VMEM((TOK, TOPK), jnp.int32),
            pltpu.VMEM((TOK, TOPK), BF16),
            sems((8,)),
            pltpu.VMEM((WIDTH, 2 * PAD), BF16),
            pltpu.VMEM((2 * PAD, WIDTH), BF16),
            pltpu.VMEM((PAD, WIDTH), BF16),
            pltpu.VMEM((WIDTH, PAD), BF16),
            pltpu.VMEM((COLS, BLOCK, LANES), BF16),
            pltpu.VMEM((BLOCK, SLOT_ROWS), BF16),
            pltpu.VMEM((SLOT_ROWS, BLOCK), BF16),
            pltpu.VMEM((BLOCK, SLOT_ROWS), BF16),
            pltpu.VMEM((SLOT_ROWS, BLOCK), BF16),
            pltpu.VMEM((SLOT_ROWS, LANES), BF16),
            pltpu.VMEM((SLOT_ROWS, LANES), BF16),
            pltpu.VMEM((SLOT_ROWS, LANES), F32),
            pltpu.VMEM((CHUNK, WIDTH), BF16),
            pltpu.VMEM((YS + 1, XS, 2, MINE, 2 * PAD), BF16),
            pltpu.VMEM((YS + 1, XS, MINE, 2 * PAD), BF16),
            pltpu.VMEM((YS + 1, XS, MINE, 2 * PAD), BF16),
            pltpu.VMEM((YS + 1, XS, MINE, 2 * PAD), BF16),
            pltpu.VMEM((YS + 1, CHUNK, PAD), BF16),
            pltpu.VMEM((MINE, 2 * PAD), F32),
            pltpu.VMEM((ZS, BLOCK, LANES), F32),
            pltpu.VMEM((YS - 1, ZS, BLOCK, LANES), BF16),
            pltpu.VMEM((ZS, YS - 1, BLOCK, LANES), BF16),
            pltpu.VMEM((ZS, BLOCK, LANES), BF16),
            pltpu.VMEM((ZS, BLOCK, LANES), BF16),
            pltpu.VMEM((SLOT_ROWS, LANES), BF16),
            pltpu.VMEM((SLOT_ROWS, LANES), BF16),
            pltpu.VMEM((SLOT_ROWS, LANES), BF16),
            pltpu.VMEM((SLOT_ROWS, LANES), BF16),
            pltpu.VMEM((CHUNK, PAD), BF16),
            pltpu.VMEM((ROWS, MINE, PAD), BF16),
            pltpu.VMEM((CHUNK, 2 * PAD), BF16),
            pltpu.VMEM((SLOT_ROWS, LANES), BF16),
            pltpu.VMEM((SLOT_ROWS, LANES), BF16),
            sems,
            sems((ZS,)),
            sems,
            sems((YS,)),
            sems((4,)),
            sems((4,)),
            sems((YS + 1,)),
            sems((YS + 1,)),
            sems((YS + 2,)),
            sems((YS + 2,)),
            sems((YS + 2,)),
            sems((YS + 2,)),
            sems,
            sems((ZS,)),
            sems,
            sems,
            pltpu.SemaphoreType.REGULAR,
        ],
        compiler_params=pltpu.CompilerParams(
            collective_id=0, has_side_effects=True, vmem_limit_bytes=64 * 2**20
        ),
    )(teacher, student, gate.T, up.T, down, ids, slots, routes)


def solution(mesh):
    return jax.shard_map(
        shards,
        mesh=mesh,
        in_specs=(
            P("col", "row"),
            P("col", "row"),
            P("row", "col"),
            P("row", "col"),
            P("col", "row"),
            P("col", None),
            P("col", None),
            P("col", None),
        ),
        out_specs=(P("col", "row"), P("col", "row"), P("col", "row")),
        check_vma=False,
    )
```

```python
import functools

import jax
import jax.numpy as jnp
from jax import lax
from jax.experimental import pallas as pl
from jax.experimental.pallas import tpu as pltpu
from jax.sharding import PartitionSpec as P

MESH = pl.DeviceIdType.MESH
F32 = jnp.float32
BF16 = jnp.bfloat16

ROWS = 8
XS = 4
YS, ZS = 4, 16
COLS = YS * ZS
TOK = 8
WIDTH = 1024
LANES = 128
SUB = WIDTH // LANES
UNITS = 462
PAD = 512
CAP = 2
TOPK = 6
SLOTS = COLS * CAP
CHUNK = ZS * TOK
MINE = CHUNK // ROWS
BLOCK = TOK * SUB
MSG = CAP * SUB
SLOT_ROWS = COLS * MSG
STUDENT = YS
Y_OFFSETS = (0, 1, 3, 2)
HALVES = ((1, 3), (2, 0))
LINE = ZS * MSG
TILE = 256


def dot(a, b):
    return jnp.dot(a, b, preferred_element_type=F32)


def to_lane_rows(rows):
    return jnp.concatenate([rows[:, j * LANES : (j + 1) * LANES] for j in range(SUB)], axis=0)


def from_lane_rows(block):
    return jnp.concatenate([block[j * TOK : (j + 1) * TOK, :] for j in range(SUB)], axis=1)


def kernel(
    teacher_hbm,
    student_hbm,
    gate_hbm,
    up_hbm,
    down_hbm,
    ids_hbm,
    slots_hbm,
    routes_hbm,
    teacher_out,
    student_out,
    input_grad,
    teacher_ref,
    student_ref,
    gate_in,
    up_in,
    down_in,
    ids_ref,
    slots_ref,
    routes_ref,
    input_sem,
    wide,
    wide_t,
    down,
    down_t,
    tokens,
    placing,
    placing_t,
    weighting,
    weighting_t,
    sent_slots,
    got_slots,
    spread,
    rows_in,
    part,
    pair,
    pair_got,
    part_got,
    hidden,
    pre,
    own_sum,
    y_send,
    y_got,
    z_send,
    z_got,
    back_send,
    back_got,
    loss_send,
    loss_got,
    grad_in,
    hid_part,
    hid_got,
    grads,
    last_send,
    last_got,
    zg_send_sem,
    zg_recv_sem,
    yf_send_sem,
    yf_recv_sem,
    a2a_send_sem,
    a2a_recv_sem,
    pair_send_sem,
    pair_recv_sem,
    rs_send_sem,
    rs_recv_sem,
    ag_send_sem,
    ag_recv_sem,
    yr_send_sem,
    yr_recv_sem,
    zr_send_sem,
    zr_recv_sem,
    ready_sem,
):
    r = lax.axis_index("row")
    c = lax.axis_index("col")
    x, core = r // 2, lax.rem(r, 2)
    y, z = c // ZS, lax.rem(c, ZS)

    def row_peer(m):
        return lax.rem(x + 1 + m // 2, 4) * 2 + lax.rem(core + 1 + lax.rem(m, 2), 2)

    def far_first(i):
        distance = ZS // 2 - (i + 1) // 2
        return lax.rem(z + distance * (1 - 2 * lax.rem(i + 1, 2)) + ZS, ZS)

    def col_peer(m):
        return lax.rem(y + 1 + lax.rem(m, YS), YS) * ZS + far_first(m // YS)

    def send(src, dst, send_sem, recv_sem, row, col):
        return pltpu.make_async_remote_copy(
            src_ref=src,
            dst_ref=dst,
            send_sem=send_sem,
            recv_sem=recv_sem,
            device_id=(row, col),
            device_id_type=MESH,
        )

    def wait_for(view, sem):
        pltpu.make_async_copy(view, view, sem).wait()

    owed, left = {}, []

    def owe(name, arrive, leave):
        owed[name] = lambda: wait_for(*arrive)
        left.append(lambda: wait_for(*leave))

    def take(*name):
        owed.pop(name)()

    inputs = [
        pltpu.make_async_copy(a, b, input_sem.at[i])
        for i, (a, b) in enumerate(
            (
                (teacher_hbm, teacher_ref),
                (student_hbm, student_ref),
                (ids_hbm, ids_ref),
                (slots_hbm, slots_ref),
                (routes_hbm, routes_ref),
                (gate_hbm, gate_in),
                (up_hbm, up_in),
                (down_hbm, down_in),
            )
        )
    ]
    for copy in inputs:
        copy.start()
    barrier = pltpu.get_barrier_semaphore()

    @pl.loop(0, ZS - 1)
    def _(i):
        to = y * ZS + far_first(i)
        pl.semaphore_signal(barrier, inc=1, device_id=(r, to), device_id_type=MESH)

    for o in range(1, YS):
        to = lax.rem(y + o, YS) * ZS + z
        pl.semaphore_signal(barrier, inc=1, device_id=(r, to), device_id_type=MESH)

    @pl.loop(0, ROWS - 1)
    def _(m):
        pl.semaphore_signal(barrier, inc=1, device_id=(row_peer(m), c), device_id_type=MESH)

    for copy in inputs[:5]:
        copy.wait()
    tokens[c] = to_lane_rows(teacher_ref[...].astype(F32)).astype(BF16)

    for ref, first in ((wide_t, 0), (wide_t, PAD), (down, 0)):
        ref[first + PAD - 64 : first + PAD, :] = jnp.zeros((64, WIDTH), BF16)
    for copy in inputs[5:]:
        copy.wait()
    wide_t[:UNITS, :] = gate_in[...]
    wide_t[PAD : PAD + UNITS, :] = up_in[...]
    down[:UNITS, :] = down_in[...]

    @pl.loop(0, 2 * PAD // TILE)
    def _(i):
        units = pl.ds(pl.multiple_of(i * TILE, TILE), TILE)
        for k in range(WIDTH // TILE):
            wide[k * TILE : (k + 1) * TILE, units] = wide_t[units, k * TILE : (k + 1) * TILE].T

    targets = (ids_ref[...] * CAP + slots_ref[...]).astype(F32)
    choices = jnp.concatenate([targets, routes_ref[...].astype(F32)], axis=1)
    choices = jnp.concatenate([choices, jnp.zeros((TOK, LANES - 2 * TOPK), F32)], axis=1)
    choices = jnp.concatenate([choices] * SUB, axis=0)
    flipped = choices.T

    def match(slot_of, targets, routes, place_ref, weigh_ref, at):
        place = jnp.zeros(slot_of.shape, F32)
        weigh = jnp.zeros(slot_of.shape, F32)
        for k in range(TOPK):
            hit = slot_of == targets(k)
            place = jnp.where(hit, 1.0, place)
            weigh = jnp.where(hit, routes(k), weigh)
        place_ref[at] = place.astype(BF16)
        weigh_ref[at] = weigh.astype(BF16)

    for i in range(SLOT_ROWS // LANES):
        shape = (BLOCK, LANES)
        row = lax.broadcasted_iota(jnp.int32, shape, 0)
        col = lax.broadcasted_iota(jnp.int32, shape, 1) + i * LANES
        slot_of = jnp.where((col & (SUB - 1)) == (row >> 3), col >> 3, -1).astype(F32)
        match(
            slot_of,
            lambda k: choices[:, k : k + 1],
            lambda k: choices[:, TOPK + k : TOPK + k + 1],
            placing,
            weighting,
            (slice(None), slice(i * LANES, (i + 1) * LANES)),
        )
        shape = (LANES, BLOCK)
        row = lax.broadcasted_iota(jnp.int32, shape, 0) + i * LANES
        col = lax.broadcasted_iota(jnp.int32, shape, 1)
        slot_of = jnp.where((row & (SUB - 1)) == (col >> 3), row >> 3, -1).astype(F32)
        match(
            slot_of,
            lambda k: flipped[k : k + 1, :],
            lambda k: flipped[TOPK + k : TOPK + k + 1, :],
            placing_t,
            weighting_t,
            (slice(i * LANES, (i + 1) * LANES), slice(None)),
        )
    student_rows = to_lane_rows(student_ref[...].astype(F32)).astype(BF16)
    sent_slots[...] = dot(placing_t[...], student_rows).astype(BF16)

    pl.semaphore_wait(barrier, ZS + YS - 2 + ROWS - 1)

    def gather_z(i):
        to = y * ZS + lax.rem(z + i, ZS)
        return send(tokens.at[c], tokens.at[c], zg_send_sem, zg_recv_sem.at[z], r, to)

    for o in [1, 15, 2, 14, 3, 13, 4, 12, 5, 11, 6, 10, 7, 9, 8]:
        gather_z(o).start()

    def forward_y(zi):
        block = tokens.at[y * ZS + zi]
        for o in (2, 1, 3):
            to = lax.rem(y + o, YS) * ZS + z
            send(block, block, yf_send_sem, yf_recv_sem.at[YS - o], r, to).start()

    left.append(lambda: wait_for(tokens.at[pl.ds(0, ZS - 1)], zg_send_sem))
    left.append(lambda: wait_for(tokens.at[pl.ds(0, 3 * ZS)], yf_send_sem))
    forward_y(z)

    for o in range(1, YS):
        to = lax.rem(y + o, YS) * ZS + z
        pl.semaphore_signal(ready_sem, inc=1, device_id=(r, to), device_id_type=MESH)
    pl.semaphore_wait(ready_sem, YS - 1)

    def all_to_all(n, src, dst):
        @pl.loop(0, COLS - 1)
        def _(m):
            to = col_peer(m)
            send(
                src.at[pl.ds(pl.multiple_of(to * MSG, MSG), MSG)],
                dst.at[pl.ds(pl.multiple_of(c * MSG, MSG), MSG)],
                a2a_send_sem.at[n],
                a2a_recv_sem.at[n],
                r,
                to,
            ).start()

        own = pl.ds(pl.multiple_of(c * MSG, MSG), MSG)
        dst[own, :] = src[own, :]
        most = pl.ds(0, (COLS - 1) * MSG)
        owe(("slots", n), (dst.at[most], a2a_recv_sem.at[n]), (src.at[most], a2a_send_sem.at[n]))

    for o in [1, 15, 2, 14, 3, 13, 4, 12, 5, 11, 6, 10, 7, 9, 8]:
        zi = lax.rem(z + o, ZS)
        block = tokens.at[y * ZS + zi]
        wait_for(block, zg_recv_sem.at[zi])
        forward_y(zi)

    all_to_all(0, sent_slots, got_slots)

    for n in range(1, YS):
        group = lax.rem(y + Y_OFFSETS[n], YS)
        block = tokens.at[pl.ds(group * ZS, ZS)]
        owed["tokens", n] = functools.partial(wait_for, block, yf_recv_sem.at[Y_OFFSETS[n]])


    def group_rows(h, i):
        return pl.multiple_of(lax.rem(y + HALVES[h][i], YS) * LINE, LINE)

    def exchange_half(n, h, src, dst):
        count = 2 * ZS - h

        @pl.loop(0, count)
        def _(m):
            to = lax.rem(y + 1 + h + 2 * lax.rem(m, 2), YS) * ZS + far_first(m // 2)
            send(
                src.at[pl.ds(pl.multiple_of(to * MSG, MSG), MSG)],
                dst.at[pl.ds(pl.multiple_of(c * MSG, MSG), MSG)],
                a2a_send_sem.at[n],
                a2a_recv_sem.at[n],
                r,
                to,
            ).start()

        if h == 1:
            own = pl.ds(pl.multiple_of(c * MSG, MSG), MSG)
            dst[own, :] = src[own, :]
        most = pl.ds(0, count * MSG)
        owe(("slots", n), (dst.at[most], a2a_recv_sem.at[n]), (src.at[most], a2a_send_sem.at[n]))

    def half_rows(h, j):
        parts = [spread[pl.ds(group_rows(h, i) + j, LINE // SUB, stride=SUB), :] for i in range(2)]
        return jnp.concatenate(parts, axis=0)

    def store_half(h, j, value):
        for i in range(2):
            rows = pl.ds(group_rows(h, i) + j, LINE // SUB, stride=SUB)
            spread[rows, :] = value[i * (LINE // SUB) : (i + 1) * (LINE // SUB), :]

    def send_rows(n, src, dst):
        @pl.loop(0, ROWS - 1)
        def _(m):
            to = row_peer(m)
            send(src.at[to], dst.at[r], rs_send_sem.at[n], rs_recv_sem.at[n], to, c).start()

        dst[r] = src[r]
        most = pl.ds(0, ROWS - 1)
        owe(("sum", n), (dst.at[most], rs_recv_sem.at[n]), (src.at[most], rs_send_sem.at[n]))

    def sum_rows(n, dst):
        take("sum", n)
        total = dst[0].astype(F32)
        for i in range(1, dst.shape[0]):
            total = total + dst[i].astype(F32)
        return total

    def gather_rows(n, buf, rows):
        mine = pl.ds(pl.multiple_of(r * MINE, MINE), MINE)
        buf[mine, :] = rows

        @pl.loop(0, ROWS - 1)
        def _(m):
            send(
                buf.at[mine], buf.at[mine], ag_send_sem.at[n], ag_recv_sem.at[n], row_peer(m), c
            ).start()

        most = buf.at[pl.ds(0, (ROWS - 1) * MINE)]
        owe(("gather", n), (most, ag_recv_sem.at[n]), (most, ag_send_sem.at[n]))

    def project(n):
        @pl.loop(0, 2 * PAD // TILE)
        def _(i):
            cols = pl.ds(pl.multiple_of(i * TILE, TILE), TILE)
            value = dot(rows_in[...], wide[:, cols]).reshape(XS, 2, MINE, TILE)
            part[n, :, :, :, cols] = value.astype(BF16)

        other = part.at[n, :, 1 - core]
        got = pair_got.at[n]
        send(other, got, pair_send_sem.at[n], pair_recv_sem.at[n], x * 2 + 1 - core, c).start()
        owe(("pair", n), (got, pair_recv_sem.at[n]), (got, pair_send_sem.at[n]))

    def combine(n):
        take("pair", n)
        pair[n] = (part[n, :, core].astype(F32) + pair_got[n].astype(F32)).astype(BF16)
        for o in (2, 1, 3):
            to = lax.rem(x + o, XS)
            send(
                pair.at[n, to],
                part_got.at[n, x],
                rs_send_sem.at[n],
                rs_recv_sem.at[n],
                to * 2 + core,
                c,
            ).start()
        part_got[n, x] = pair[n, x]
        most = pl.ds(0, XS - 1)
        owe(
            ("sum", n),
            (part_got.at[n, most], rs_recv_sem.at[n]),
            (pair.at[n, most], rs_send_sem.at[n]),
        )

    def load_teacher(n):
        group = lax.rem(y + Y_OFFSETS[n], YS)
        if n > 0:
            take("tokens", n)
        blocks = tokens[pl.ds(group * ZS, ZS)].astype(F32).reshape(ZS, SUB, TOK, LANES)
        for j in range(SUB):
            rows_in[:, j * LANES : (j + 1) * LANES] = (
                blocks[:, j].reshape(CHUNK, LANES).astype(BF16)
            )

    def load_slots(got):
        spread[...] = got[...].astype(F32)
        for j in range(SUB):
            halves = [half_rows(h, j).reshape(ROWS, SUB, LANES) for h in range(2)]
            rows_in[:, j * LANES : (j + 1) * LANES] = (
                jnp.concatenate(halves, axis=1).reshape(SLOTS, LANES).astype(BF16)
            )

    def activate(n):
        total = sum_rows(n, part_got.at[n])
        gate, up = total[:, :PAD], total[:, PAD:]
        if n == STUDENT:
            pre[...] = total
        gather_rows(n, hidden.at[n], (gate / (1.0 + jnp.exp(-gate)) * up).astype(BF16))

    def store_slots(value, first):
        for j in range(TILE // LANES):
            rows = value[:, j * LANES : (j + 1) * LANES].reshape(ROWS, 2, SUB, LANES)
            for h in range(2):
                store_half(h, first + j, rows[:, h].reshape(SLOTS // 2, LANES))

    def produce_teacher(n):
        take("gather", n)
        for i in range(WIDTH // TILE):
            value = dot(hidden[n], down[:, i * TILE : (i + 1) * TILE])
            halves = [
                value[:, j * LANES : (j + 1) * LANES].reshape(ZS, TOK, LANES)
                for j in range(TILE // LANES)
            ]
            value = jnp.concatenate(halves, axis=1)
            rows = slice(i * 2 * TOK, (i + 1) * 2 * TOK)
            if n == 0:
                own_sum[:, rows, :] = value
            else:
                y_send[n - 1, :, rows, :] = value.astype(BF16)
        if n > 0:
            o = Y_OFFSETS[n]
            to = lax.rem(y + o, YS) * ZS + z
            left.append(lambda: wait_for(y_send.at[n - 1], yr_send_sem))

            @pl.loop(0, ZS)
            def _(i):
                zi = far_first(i)
                send(
                    y_send.at[n - 1, zi],
                    y_got.at[zi, n - 1],
                    yr_send_sem,
                    yr_recv_sem.at[zi],
                    r,
                    to,
                ).start()

    def produce_student():
        take("gather", STUDENT)
        for i in range(WIDTH // TILE):
            value = dot(hidden[STUDENT], down[:, i * TILE : (i + 1) * TILE])
            store_slots(value, i * (TILE // LANES))
        back_send[...] = spread[...].astype(BF16)
        all_to_all(1, back_send, back_got)

    load_teacher(0)
    project(0)
    load_teacher(1)
    project(1)
    combine(0)
    load_teacher(2)
    project(2)
    combine(1)
    load_teacher(3)
    project(3)
    combine(2)
    activate(0)
    combine(3)
    activate(1)
    take("slots", 0)
    load_slots(got_slots)
    project(STUDENT)
    activate(2)
    combine(STUDENT)
    activate(3)
    produce_teacher(1)
    produce_teacher(2)
    activate(STUDENT)
    produce_teacher(3)
    produce_student()
    produce_teacher(0)

    @pl.loop(0, ZS)
    def _(i):
        zi = far_first(i)
        wait_for(y_got.at[zi], yr_recv_sem.at[zi])
        got = y_got[zi].astype(F32)
        total = own_sum[zi] + got[0] + got[1] + got[2]
        z_send[zi] = total.astype(BF16)

        @pl.when(i < ZS - 1)
        def _():
            to = y * ZS + zi
            send(z_send.at[zi], z_got.at[z], zr_send_sem, zr_recv_sem, r, to).start()

        @pl.when(i == ZS - 1)
        def _():
            z_got[zi] = total.astype(BF16)

    left.append(lambda: wait_for(z_send.at[pl.ds(0, ZS - 1)], zr_send_sem))

    @pl.loop(0, PAD // TILE)
    def _(i):
        units = pl.ds(pl.multiple_of(i * TILE, TILE), TILE)
        for k in range(WIDTH // TILE):
            down_t[k * TILE : (k + 1) * TILE, units] = down[units, k * TILE : (k + 1) * TILE].T

    wait_for(z_got.at[pl.ds(0, ZS - 1)], zr_recv_sem)
    teacher = z_got[0].astype(F32)
    for i in range(1, ZS):
        teacher = teacher + z_got[i].astype(F32)
    teacher = teacher.astype(BF16).astype(F32)
    teacher_out[...] = from_lane_rows(teacher).astype(BF16)

    take("slots", 1)
    student = dot(weighting[...], back_got[...]).astype(BF16).astype(F32)
    loss = (student - teacher).astype(BF16)
    loss_send[...] = dot(weighting_t[...], loss).astype(BF16)
    for h in range(2):
        exchange_half(2 + h, h, loss_send, loss_got)
    student_out[...] = from_lane_rows(student).astype(BF16)
    pre_gate, pre_up = pre[:, :PAD], pre[:, PAD:]
    logistic = 1.0 / (1.0 + jnp.exp(-pre_gate))
    pre[:, PAD:] = pre_up * (logistic * (1.0 + pre_gate * (1.0 - logistic)))
    pre[:, :PAD] = pre_gate * logistic

    def hidden_half(h):
        take("slots", 2 + h)
        for i in range(2):
            rows = pl.ds(group_rows(h, i), LINE)
            spread[rows, :] = loss_got[rows, :].astype(F32)
        for j in range(SUB):
            grad_in[:, j * LANES : (j + 1) * LANES] = half_rows(h, j).astype(BF16)
        for i in range(PAD // TILE):
            value = dot(grad_in[...], down_t[:, i * TILE : (i + 1) * TILE])
            parts = [
                value[:, j * LANES : (j + 1) * LANES].reshape(ROWS, SUB, LANES)
                for j in range(TILE // LANES)
            ]
            rows = slice(i * 2 * SUB, (i + 1) * 2 * SUB)
            hid_part[h, :, rows, :] = jnp.concatenate(parts, axis=1).astype(BF16)
        send_rows(YS + 1 + h, hid_part.at[h], hid_got.at[h])

    def grads_half(h):
        n = YS + 1 + h
        total = sum_rows(n, hid_got.at[h])
        parts = [total[j * SUB : (j + 1) * SUB, :] for j in range(PAD // LANES)]
        hidden_grad = jnp.concatenate(parts, axis=1)
        mine = slice(h * SUB, (h + 1) * SUB)
        gate_grad = hidden_grad * pre[mine, PAD:]
        up_grad = hidden_grad * pre[mine, :PAD]
        both = jnp.concatenate([gate_grad, up_grad], axis=1)
        grads[h, r] = to_lane_rows(both).astype(BF16)

        @pl.loop(0, ROWS - 1)
        def _(m):
            block = grads.at[h, r]
            send(block, block, ag_send_sem.at[n], ag_recv_sem.at[n], row_peer(m), c).start()

        most = grads.at[h, pl.ds(0, ROWS - 1)]
        owe(("gather", n), (most, ag_recv_sem.at[n]), (most, ag_send_sem.at[n]))

    def rows_half(h):
        take("gather", YS + 1 + h)
        blocks = grads[h].astype(F32).reshape(ROWS, SUB, SUB, LANES)
        for j in range(SUB):
            grad_in[:, j * LANES : (j + 1) * LANES] = (
                blocks[:, j].reshape(SLOTS // 2, LANES).astype(BF16)
            )
        for i in range(WIDTH // TILE):
            value = dot(grad_in[...], wide_t[:, i * TILE : (i + 1) * TILE])
            for j in range(TILE // LANES):
                at = i * (TILE // LANES) + j
                store_half(h, at, value[:, j * LANES : (j + 1) * LANES])
        for i in range(2):
            rows = pl.ds(group_rows(h, i), LINE)
            last_send[rows, :] = spread[rows, :].astype(BF16)
        exchange_half(4 + h, h, last_send, last_got)

    hidden_half(0)
    grads_half(0)
    hidden_half(1)
    rows_half(0)
    grads_half(1)
    rows_half(1)
    take("slots", 4)
    take("slots", 5)
    grad = dot(placing[...], last_got[...])
    input_grad[...] = from_lane_rows(grad).astype(BF16)

    for wait in left:
        wait()


def shards(teacher, student, gate, up, down, ids, slots, routes):
    vmem = pl.BlockSpec(memory_space=pltpu.VMEM)
    hbm = pl.BlockSpec(memory_space=pltpu.HBM)
    out = jax.ShapeDtypeStruct((TOK, WIDTH), BF16)
    sems = pltpu.SemaphoreType.DMA
    return pl.pallas_call(
        kernel,
        out_shape=(out, out, out),
        in_specs=[hbm] * 8,
        out_specs=(vmem, vmem, vmem),
        scratch_shapes=[
            pltpu.VMEM((TOK, WIDTH), BF16),
            pltpu.VMEM((TOK, WIDTH), BF16),
            pltpu.VMEM((UNITS, WIDTH), BF16),
            pltpu.VMEM((UNITS, WIDTH), BF16),
            pltpu.VMEM((UNITS, WIDTH), BF16),
            pltpu.VMEM((TOK, TOPK), jnp.int32),
            pltpu.VMEM((TOK, TOPK), jnp.int32),
            pltpu.VMEM((TOK, TOPK), BF16),
            sems((8,)),
            pltpu.VMEM((WIDTH, 2 * PAD), BF16),
            pltpu.VMEM((2 * PAD, WIDTH), BF16),
            pltpu.VMEM((PAD, WIDTH), BF16),
            pltpu.VMEM((WIDTH, PAD), BF16),
            pltpu.VMEM((COLS, BLOCK, LANES), BF16),
            pltpu.VMEM((BLOCK, SLOT_ROWS), BF16),
            pltpu.VMEM((SLOT_ROWS, BLOCK), BF16),
            pltpu.VMEM((BLOCK, SLOT_ROWS), BF16),
            pltpu.VMEM((SLOT_ROWS, BLOCK), BF16),
            pltpu.VMEM((SLOT_ROWS, LANES), BF16),
            pltpu.VMEM((SLOT_ROWS, LANES), BF16),
            pltpu.VMEM((SLOT_ROWS, LANES), F32),
            pltpu.VMEM((CHUNK, WIDTH), BF16),
            pltpu.VMEM((YS + 1, XS, 2, MINE, 2 * PAD), BF16),
            pltpu.VMEM((YS + 1, XS, MINE, 2 * PAD), BF16),
            pltpu.VMEM((YS + 1, XS, MINE, 2 * PAD), BF16),
            pltpu.VMEM((YS + 1, XS, MINE, 2 * PAD), BF16),
            pltpu.VMEM((YS + 1, CHUNK, PAD), BF16),
            pltpu.VMEM((MINE, 2 * PAD), F32),
            pltpu.VMEM((ZS, BLOCK, LANES), F32),
            pltpu.VMEM((YS - 1, ZS, BLOCK, LANES), BF16),
            pltpu.VMEM((ZS, YS - 1, BLOCK, LANES), BF16),
            pltpu.VMEM((ZS, BLOCK, LANES), BF16),
            pltpu.VMEM((ZS, BLOCK, LANES), BF16),
            pltpu.VMEM((SLOT_ROWS, LANES), BF16),
            pltpu.VMEM((SLOT_ROWS, LANES), BF16),
            pltpu.VMEM((SLOT_ROWS, LANES), BF16),
            pltpu.VMEM((SLOT_ROWS, LANES), BF16),
            pltpu.VMEM((SLOTS // 2, WIDTH), BF16),
            pltpu.VMEM((2, ROWS, PAD // LANES * SUB, LANES), BF16),
            pltpu.VMEM((2, ROWS, PAD // LANES * SUB, LANES), BF16),
            pltpu.VMEM((2, ROWS, 2 * PAD // LANES * SUB, LANES), BF16),
            pltpu.VMEM((SLOT_ROWS, LANES), BF16),
            pltpu.VMEM((SLOT_ROWS, LANES), BF16),
            sems,
            sems((ZS,)),
            sems,
            sems((YS,)),
            sems((6,)),
            sems((6,)),
            sems((YS + 1,)),
            sems((YS + 1,)),
            sems((YS + 3,)),
            sems((YS + 3,)),
            sems((YS + 3,)),
            sems((YS + 3,)),
            sems,
            sems((ZS,)),
            sems,
            sems,
            pltpu.SemaphoreType.REGULAR,
        ],
        compiler_params=pltpu.CompilerParams(
            collective_id=0, has_side_effects=True, vmem_limit_bytes=64 * 2**20
        ),
    )(teacher, student, gate.T, up.T, down, ids, slots, routes)


def solution(mesh):
    return jax.shard_map(
        shards,
        mesh=mesh,
        in_specs=(
            P("col", "row"),
            P("col", "row"),
            P("row", "col"),
            P("row", "col"),
            P("col", "row"),
            P("col", None),
            P("col", None),
            P("col", None),
        ),
        out_specs=(P("col", "row"), P("col", "row"), P("col", "row")),
        check_vma=False,
    )
```

```python
import functools

import jax
import jax.numpy as jnp
from jax import lax
from jax.experimental import pallas as pl
from jax.experimental.pallas import tpu as pltpu
from jax.sharding import PartitionSpec as P

MESH = pl.DeviceIdType.MESH
F32 = jnp.float32
BF16 = jnp.bfloat16

ROWS = 8
XS = 4
YS, ZS = 4, 16
COLS = YS * ZS
TOK = 8
WIDTH = 1024
LANES = 128
SUB = WIDTH // LANES
UNITS = 462
PAD = 512
CAP = 2
TOPK = 6
SLOTS = COLS * CAP
CHUNK = ZS * TOK
MINE = CHUNK // ROWS
BLOCK = TOK * SUB
MSG = CAP * SUB
SLOT_ROWS = COLS * MSG
STUDENT = YS
Y_OFFSETS = (0, 2, 1, 3)
HALVES = ((1, 3), (2, 0))
LINE = ZS * MSG
TILE = 256


def dot(a, b):
    return jnp.dot(a, b, preferred_element_type=F32)


def to_lane_rows(rows):
    return jnp.concatenate([rows[:, j * LANES : (j + 1) * LANES] for j in range(SUB)], axis=0)


def from_lane_rows(block):
    return jnp.concatenate([block[j * TOK : (j + 1) * TOK, :] for j in range(SUB)], axis=1)


def kernel(
    teacher_hbm,
    student_hbm,
    gate_hbm,
    up_hbm,
    down_hbm,
    ids_hbm,
    slots_hbm,
    routes_hbm,
    teacher_out,
    student_out,
    input_grad,
    teacher_ref,
    student_ref,
    gate_in,
    up_in,
    down_in,
    ids_ref,
    slots_ref,
    routes_ref,
    input_sem,
    wide,
    wide_t,
    down,
    down_t,
    tokens,
    placing,
    placing_t,
    weighting,
    weighting_t,
    sent_slots,
    got_slots,
    spread,
    rows_in,
    part,
    pair,
    pair_got,
    part_got,
    hidden,
    pre,
    own_sum,
    y_send,
    y_got,
    z_send,
    z_got,
    back_send,
    back_got,
    loss_send,
    loss_got,
    grad_in,
    hid_part,
    hid_got,
    grads,
    last_send,
    last_got,
    zg_send_sem,
    zg_recv_sem,
    yf_send_sem,
    yf_recv_sem,
    a2a_send_sem,
    a2a_recv_sem,
    pair_send_sem,
    pair_recv_sem,
    rs_send_sem,
    rs_recv_sem,
    ag_send_sem,
    ag_recv_sem,
    yr_send_sem,
    yr_recv_sem,
    zr_send_sem,
    zr_recv_sem,
    ready_sem,
):
    r = lax.axis_index("row")
    c = lax.axis_index("col")
    x, core = r // 2, lax.rem(r, 2)
    y, z = c // ZS, lax.rem(c, ZS)

    def row_peer(m):
        return lax.rem(x + 1 + m // 2, 4) * 2 + lax.rem(core + 1 + lax.rem(m, 2), 2)

    def far_first(i):
        distance = ZS // 2 - (i + 1) // 2
        return lax.rem(z + distance * (1 - 2 * lax.rem(i + 1, 2)) + ZS, ZS)

    def col_peer(m):
        return lax.rem(y + 1 + lax.rem(m, YS), YS) * ZS + far_first(m // YS)

    def send(src, dst, send_sem, recv_sem, row, col):
        return pltpu.make_async_remote_copy(
            src_ref=src,
            dst_ref=dst,
            send_sem=send_sem,
            recv_sem=recv_sem,
            device_id=(row, col),
            device_id_type=MESH,
        )

    def wait_for(view, sem):
        pltpu.make_async_copy(view, view, sem).wait()

    owed, left = {}, []

    def owe(name, arrive, leave):
        owed[name] = lambda: wait_for(*arrive)
        left.append(lambda: wait_for(*leave))

    def take(*name):
        owed.pop(name)()

    inputs = [
        pltpu.make_async_copy(a, b, input_sem.at[i])
        for i, (a, b) in enumerate(
            (
                (teacher_hbm, teacher_ref),
                (student_hbm, student_ref),
                (ids_hbm, ids_ref),
                (slots_hbm, slots_ref),
                (routes_hbm, routes_ref),
                (gate_hbm, gate_in),
                (up_hbm, up_in),
                (down_hbm, down_in),
            )
        )
    ]
    for copy in inputs:
        copy.start()
    barrier = pltpu.get_barrier_semaphore()

    @pl.loop(0, ZS - 1)
    def _(i):
        to = y * ZS + far_first(i)
        pl.semaphore_signal(barrier, inc=1, device_id=(r, to), device_id_type=MESH)

    for o in range(1, YS):
        to = lax.rem(y + o, YS) * ZS + z
        pl.semaphore_signal(barrier, inc=1, device_id=(r, to), device_id_type=MESH)

    @pl.loop(0, ROWS - 1)
    def _(m):
        pl.semaphore_signal(barrier, inc=1, device_id=(row_peer(m), c), device_id_type=MESH)

    for copy in inputs[:5]:
        copy.wait()
    tokens[c] = to_lane_rows(teacher_ref[...].astype(F32)).astype(BF16)

    for ref, first in ((wide_t, 0), (wide_t, PAD), (down, 0)):
        ref[first + PAD - 64 : first + PAD, :] = jnp.zeros((64, WIDTH), BF16)
    for copy in inputs[5:]:
        copy.wait()
    wide_t[:UNITS, :] = gate_in[...]
    wide_t[PAD : PAD + UNITS, :] = up_in[...]
    down[:UNITS, :] = down_in[...]

    @pl.loop(0, 2 * PAD // TILE)
    def _(i):
        units = pl.ds(pl.multiple_of(i * TILE, TILE), TILE)
        for k in range(WIDTH // TILE):
            wide[k * TILE : (k + 1) * TILE, units] = wide_t[units, k * TILE : (k + 1) * TILE].T

    targets = (ids_ref[...] * CAP + slots_ref[...]).astype(F32)
    choices = jnp.concatenate([targets, routes_ref[...].astype(F32)], axis=1)
    choices = jnp.concatenate([choices, jnp.zeros((TOK, LANES - 2 * TOPK), F32)], axis=1)
    choices = jnp.concatenate([choices] * SUB, axis=0)
    flipped = choices.T

    def match(slot_of, targets, routes, place_ref, weigh_ref, at):
        place = jnp.zeros(slot_of.shape, F32)
        weigh = jnp.zeros(slot_of.shape, F32)
        for k in range(TOPK):
            hit = slot_of == targets(k)
            place = jnp.where(hit, 1.0, place)
            weigh = jnp.where(hit, routes(k), weigh)
        place_ref[at] = place.astype(BF16)
        weigh_ref[at] = weigh.astype(BF16)

    for i in range(SLOT_ROWS // LANES):
        shape = (BLOCK, LANES)
        row = lax.broadcasted_iota(jnp.int32, shape, 0)
        col = lax.broadcasted_iota(jnp.int32, shape, 1) + i * LANES
        slot_of = jnp.where((col & (SUB - 1)) == (row >> 3), col >> 3, -1).astype(F32)
        match(
            slot_of,
            lambda k: choices[:, k : k + 1],
            lambda k: choices[:, TOPK + k : TOPK + k + 1],
            placing,
            weighting,
            (slice(None), slice(i * LANES, (i + 1) * LANES)),
        )
        shape = (LANES, BLOCK)
        row = lax.broadcasted_iota(jnp.int32, shape, 0) + i * LANES
        col = lax.broadcasted_iota(jnp.int32, shape, 1)
        slot_of = jnp.where((row & (SUB - 1)) == (col >> 3), row >> 3, -1).astype(F32)
        match(
            slot_of,
            lambda k: flipped[k : k + 1, :],
            lambda k: flipped[TOPK + k : TOPK + k + 1, :],
            placing_t,
            weighting_t,
            (slice(i * LANES, (i + 1) * LANES), slice(None)),
        )
    student_rows = to_lane_rows(student_ref[...].astype(F32)).astype(BF16)
    sent_slots[...] = dot(placing_t[...], student_rows).astype(BF16)

    pl.semaphore_wait(barrier, ZS + YS - 2 + ROWS - 1)

    def gather_z(i):
        to = y * ZS + lax.rem(z + i, ZS)
        return send(tokens.at[c], tokens.at[c], zg_send_sem, zg_recv_sem.at[z], r, to)

    for o in [1, 15, 2, 14, 3, 13, 4, 12, 5, 11, 6, 10, 7, 9, 8]:
        gather_z(o).start()

    def forward_y(zi):
        block = tokens.at[y * ZS + zi]
        for o in (2, 1, 3):
            to = lax.rem(y + o, YS) * ZS + z
            send(block, block, yf_send_sem, yf_recv_sem.at[YS - o], r, to).start()

    left.append(lambda: wait_for(tokens.at[pl.ds(0, ZS - 1)], zg_send_sem))
    left.append(lambda: wait_for(tokens.at[pl.ds(0, 3 * ZS)], yf_send_sem))
    forward_y(z)

    for o in range(1, YS):
        to = lax.rem(y + o, YS) * ZS + z
        pl.semaphore_signal(ready_sem, inc=1, device_id=(r, to), device_id_type=MESH)
    pl.semaphore_wait(ready_sem, YS - 1)

    def all_to_all(n, src, dst):
        @pl.loop(0, COLS - 1)
        def _(m):
            to = col_peer(m)
            send(
                src.at[pl.ds(pl.multiple_of(to * MSG, MSG), MSG)],
                dst.at[pl.ds(pl.multiple_of(c * MSG, MSG), MSG)],
                a2a_send_sem.at[n],
                a2a_recv_sem.at[n],
                r,
                to,
            ).start()

        own = pl.ds(pl.multiple_of(c * MSG, MSG), MSG)
        dst[own, :] = src[own, :]
        most = pl.ds(0, (COLS - 1) * MSG)
        owe(("slots", n), (dst.at[most], a2a_recv_sem.at[n]), (src.at[most], a2a_send_sem.at[n]))

    for o in [1, 15, 2, 14, 3, 13, 4, 12, 5, 11, 6, 10, 7, 9, 8]:
        zi = lax.rem(z + o, ZS)
        block = tokens.at[y * ZS + zi]
        wait_for(block, zg_recv_sem.at[zi])
        forward_y(zi)

    all_to_all(0, sent_slots, got_slots)

    for n in range(1, YS):
        group = lax.rem(y + Y_OFFSETS[n], YS)
        block = tokens.at[pl.ds(group * ZS, ZS)]
        owed["tokens", n] = functools.partial(wait_for, block, yf_recv_sem.at[Y_OFFSETS[n]])


    def group_rows(h, i):
        return pl.multiple_of(lax.rem(y + HALVES[h][i], YS) * LINE, LINE)

    def exchange_half(n, h, src, dst):
        count = 2 * ZS - h

        @pl.loop(0, count)
        def _(m):
            to = lax.rem(y + 1 + h + 2 * lax.rem(m, 2), YS) * ZS + far_first(m // 2)
            send(
                src.at[pl.ds(pl.multiple_of(to * MSG, MSG), MSG)],
                dst.at[pl.ds(pl.multiple_of(c * MSG, MSG), MSG)],
                a2a_send_sem.at[n],
                a2a_recv_sem.at[n],
                r,
                to,
            ).start()

        if h == 1:
            own = pl.ds(pl.multiple_of(c * MSG, MSG), MSG)
            dst[own, :] = src[own, :]
        most = pl.ds(0, count * MSG)
        owe(("slots", n), (dst.at[most], a2a_recv_sem.at[n]), (src.at[most], a2a_send_sem.at[n]))

    def half_rows(h, j):
        parts = [spread[pl.ds(group_rows(h, i) + j, LINE // SUB, stride=SUB), :] for i in range(2)]
        return jnp.concatenate(parts, axis=0)

    def store_half(h, j, value):
        for i in range(2):
            rows = pl.ds(group_rows(h, i) + j, LINE // SUB, stride=SUB)
            spread[rows, :] = value[i * (LINE // SUB) : (i + 1) * (LINE // SUB), :]

    def send_rows(n, src, dst):
        @pl.loop(0, ROWS - 1)
        def _(m):
            to = row_peer(m)
            send(src.at[to], dst.at[r], rs_send_sem.at[n], rs_recv_sem.at[n], to, c).start()

        dst[r] = src[r]
        most = pl.ds(0, ROWS - 1)
        owe(("sum", n), (dst.at[most], rs_recv_sem.at[n]), (src.at[most], rs_send_sem.at[n]))

    def sum_rows(n, dst):
        take("sum", n)
        total = dst[0].astype(F32)
        for i in range(1, dst.shape[0]):
            total = total + dst[i].astype(F32)
        return total

    def gather_rows(n, buf, rows):
        mine = pl.ds(pl.multiple_of(r * MINE, MINE), MINE)
        buf[mine, :] = rows

        @pl.loop(0, ROWS - 1)
        def _(m):
            send(
                buf.at[mine], buf.at[mine], ag_send_sem.at[n], ag_recv_sem.at[n], row_peer(m), c
            ).start()

        most = buf.at[pl.ds(0, (ROWS - 1) * MINE)]
        owe(("gather", n), (most, ag_recv_sem.at[n]), (most, ag_send_sem.at[n]))

    def project(n):
        @pl.loop(0, 2 * PAD // TILE)
        def _(i):
            cols = pl.ds(pl.multiple_of(i * TILE, TILE), TILE)
            value = dot(rows_in[...], wide[:, cols]).reshape(XS, 2, MINE, TILE)
            part[n, :, :, :, cols] = value.astype(BF16)

        other = part.at[n, :, 1 - core]
        got = pair_got.at[n]
        send(other, got, pair_send_sem.at[n], pair_recv_sem.at[n], x * 2 + 1 - core, c).start()
        owe(("pair", n), (got, pair_recv_sem.at[n]), (got, pair_send_sem.at[n]))

    def combine(n):
        take("pair", n)
        pair[n] = (part[n, :, core].astype(F32) + pair_got[n].astype(F32)).astype(BF16)
        for o in (2, 1, 3):
            to = lax.rem(x + o, XS)
            send(
                pair.at[n, to],
                part_got.at[n, x],
                rs_send_sem.at[n],
                rs_recv_sem.at[n],
                to * 2 + core,
                c,
            ).start()
        part_got[n, x] = pair[n, x]
        most = pl.ds(0, XS - 1)
        owe(
            ("sum", n),
            (part_got.at[n, most], rs_recv_sem.at[n]),
            (pair.at[n, most], rs_send_sem.at[n]),
        )

    def load_teacher(n):
        group = lax.rem(y + Y_OFFSETS[n], YS)
        if n > 0:
            take("tokens", n)
        blocks = tokens[pl.ds(group * ZS, ZS)].astype(F32).reshape(ZS, SUB, TOK, LANES)
        for j in range(SUB):
            rows_in[:, j * LANES : (j + 1) * LANES] = (
                blocks[:, j].reshape(CHUNK, LANES).astype(BF16)
            )

    def load_slots(got):
        spread[...] = got[...].astype(F32)
        for j in range(SUB):
            halves = [half_rows(h, j).reshape(ROWS, SUB, LANES) for h in range(2)]
            rows_in[:, j * LANES : (j + 1) * LANES] = (
                jnp.concatenate(halves, axis=1).reshape(SLOTS, LANES).astype(BF16)
            )

    def activate(n):
        total = sum_rows(n, part_got.at[n])
        gate, up = total[:, :PAD], total[:, PAD:]
        if n == STUDENT:
            pre[...] = total
        gather_rows(n, hidden.at[n], (gate / (1.0 + jnp.exp(-gate)) * up).astype(BF16))

    def store_slots(value, first):
        for j in range(TILE // LANES):
            rows = value[:, j * LANES : (j + 1) * LANES].reshape(ROWS, 2, SUB, LANES)
            for h in range(2):
                store_half(h, first + j, rows[:, h].reshape(SLOTS // 2, LANES))

    def produce_teacher(n):
        take("gather", n)
        for i in range(WIDTH // TILE):
            value = dot(hidden[n], down[:, i * TILE : (i + 1) * TILE])
            halves = [
                value[:, j * LANES : (j + 1) * LANES].reshape(ZS, TOK, LANES)
                for j in range(TILE // LANES)
            ]
            value = jnp.concatenate(halves, axis=1)
            rows = slice(i * 2 * TOK, (i + 1) * 2 * TOK)
            if n == 0:
                own_sum[:, rows, :] = value
            else:
                y_send[n - 1, :, rows, :] = value.astype(BF16)
        if n > 0:
            o = Y_OFFSETS[n]
            to = lax.rem(y + o, YS) * ZS + z
            left.append(lambda: wait_for(y_send.at[n - 1], yr_send_sem))

            @pl.loop(0, ZS)
            def _(i):
                zi = far_first(i)
                send(
                    y_send.at[n - 1, zi],
                    y_got.at[zi, n - 1],
                    yr_send_sem,
                    yr_recv_sem.at[zi],
                    r,
                    to,
                ).start()

    def produce_student():
        take("gather", STUDENT)
        for i in range(WIDTH // TILE):
            value = dot(hidden[STUDENT], down[:, i * TILE : (i + 1) * TILE])
            store_slots(value, i * (TILE // LANES))
        back_send[...] = spread[...].astype(BF16)
        all_to_all(1, back_send, back_got)

    load_teacher(0)
    project(0)
    load_teacher(1)
    project(1)
    combine(0)
    load_teacher(2)
    project(2)
    combine(1)
    load_teacher(3)
    project(3)
    combine(2)
    activate(0)
    combine(3)
    activate(1)
    take("slots", 0)
    load_slots(got_slots)
    project(STUDENT)
    activate(2)
    combine(STUDENT)
    activate(3)
    produce_teacher(1)
    produce_teacher(2)
    activate(STUDENT)
    produce_teacher(3)
    produce_student()
    produce_teacher(0)

    @pl.loop(0, ZS)
    def _(i):
        zi = far_first(i)
        wait_for(y_got.at[zi], yr_recv_sem.at[zi])
        got = y_got[zi].astype(F32)
        total = own_sum[zi] + got[0] + got[1] + got[2]
        z_send[zi] = total.astype(BF16)

        @pl.when(i < ZS - 1)
        def _():
            to = y * ZS + zi
            send(z_send.at[zi], z_got.at[z], zr_send_sem, zr_recv_sem, r, to).start()

        @pl.when(i == ZS - 1)
        def _():
            z_got[zi] = total.astype(BF16)

    left.append(lambda: wait_for(z_send.at[pl.ds(0, ZS - 1)], zr_send_sem))

    @pl.loop(0, PAD // TILE)
    def _(i):
        units = pl.ds(pl.multiple_of(i * TILE, TILE), TILE)
        for k in range(WIDTH // TILE):
            down_t[k * TILE : (k + 1) * TILE, units] = down[units, k * TILE : (k + 1) * TILE].T

    wait_for(z_got.at[pl.ds(0, ZS - 1)], zr_recv_sem)
    teacher = z_got[0].astype(F32)
    for i in range(1, ZS):
        teacher = teacher + z_got[i].astype(F32)
    teacher = teacher.astype(BF16).astype(F32)
    teacher_out[...] = from_lane_rows(teacher).astype(BF16)

    take("slots", 1)
    student = dot(weighting[...], back_got[...]).astype(BF16).astype(F32)
    loss = (student - teacher).astype(BF16)
    loss_send[...] = dot(weighting_t[...], loss).astype(BF16)
    for h in range(2):
        exchange_half(2 + h, h, loss_send, loss_got)
    student_out[...] = from_lane_rows(student).astype(BF16)
    pre_gate, pre_up = pre[:, :PAD], pre[:, PAD:]
    logistic = 1.0 / (1.0 + jnp.exp(-pre_gate))
    pre[:, PAD:] = pre_up * (logistic * (1.0 + pre_gate * (1.0 - logistic)))
    pre[:, :PAD] = pre_gate * logistic

    def hidden_half(h):
        take("slots", 2 + h)
        for i in range(2):
            rows = pl.ds(group_rows(h, i), LINE)
            spread[rows, :] = loss_got[rows, :].astype(F32)
        for j in range(SUB):
            grad_in[:, j * LANES : (j + 1) * LANES] = half_rows(h, j).astype(BF16)
        for i in range(PAD // TILE):
            value = dot(grad_in[...], down_t[:, i * TILE : (i + 1) * TILE])
            parts = [
                value[:, j * LANES : (j + 1) * LANES].reshape(ROWS, SUB, LANES)
                for j in range(TILE // LANES)
            ]
            rows = slice(i * 2 * SUB, (i + 1) * 2 * SUB)
            hid_part[h, :, rows, :] = jnp.concatenate(parts, axis=1).astype(BF16)
        send_rows(YS + 1 + h, hid_part.at[h], hid_got.at[h])

    def grads_half(h):
        n = YS + 1 + h
        total = sum_rows(n, hid_got.at[h])
        parts = [total[j * SUB : (j + 1) * SUB, :] for j in range(PAD // LANES)]
        hidden_grad = jnp.concatenate(parts, axis=1)
        mine = slice(h * SUB, (h + 1) * SUB)
        gate_grad = hidden_grad * pre[mine, PAD:]
        up_grad = hidden_grad * pre[mine, :PAD]
        both = jnp.concatenate([gate_grad, up_grad], axis=1)
        grads[h, r] = to_lane_rows(both).astype(BF16)

        @pl.loop(0, ROWS - 1)
        def _(m):
            block = grads.at[h, r]
            send(block, block, ag_send_sem.at[n], ag_recv_sem.at[n], row_peer(m), c).start()

        most = grads.at[h, pl.ds(0, ROWS - 1)]
        owe(("gather", n), (most, ag_recv_sem.at[n]), (most, ag_send_sem.at[n]))

    def rows_half(h):
        take("gather", YS + 1 + h)
        blocks = grads[h].astype(F32).reshape(ROWS, SUB, SUB, LANES)
        for j in range(SUB):
            grad_in[:, j * LANES : (j + 1) * LANES] = (
                blocks[:, j].reshape(SLOTS // 2, LANES).astype(BF16)
            )
        for i in range(WIDTH // TILE):
            value = dot(grad_in[...], wide_t[:, i * TILE : (i + 1) * TILE])
            for j in range(TILE // LANES):
                at = i * (TILE // LANES) + j
                store_half(h, at, value[:, j * LANES : (j + 1) * LANES])
        for i in range(2):
            rows = pl.ds(group_rows(h, i), LINE)
            last_send[rows, :] = spread[rows, :].astype(BF16)
        exchange_half(4 + h, h, last_send, last_got)

    hidden_half(0)
    grads_half(0)
    hidden_half(1)
    rows_half(0)
    grads_half(1)
    rows_half(1)
    take("slots", 4)
    take("slots", 5)
    grad = dot(placing[...], last_got[...])
    input_grad[...] = from_lane_rows(grad).astype(BF16)

    for wait in left:
        wait()


def shards(teacher, student, gate, up, down, ids, slots, routes):
    vmem = pl.BlockSpec(memory_space=pltpu.VMEM)
    hbm = pl.BlockSpec(memory_space=pltpu.HBM)
    out = jax.ShapeDtypeStruct((TOK, WIDTH), BF16)
    sems = pltpu.SemaphoreType.DMA
    return pl.pallas_call(
        kernel,
        out_shape=(out, out, out),
        in_specs=[hbm] * 8,
        out_specs=(vmem, vmem, vmem),
        scratch_shapes=[
            pltpu.VMEM((TOK, WIDTH), BF16),
            pltpu.VMEM((TOK, WIDTH), BF16),
            pltpu.VMEM((UNITS, WIDTH), BF16),
            pltpu.VMEM((UNITS, WIDTH), BF16),
            pltpu.VMEM((UNITS, WIDTH), BF16),
            pltpu.VMEM((TOK, TOPK), jnp.int32),
            pltpu.VMEM((TOK, TOPK), jnp.int32),
            pltpu.VMEM((TOK, TOPK), BF16),
            sems((8,)),
            pltpu.VMEM((WIDTH, 2 * PAD), BF16),
            pltpu.VMEM((2 * PAD, WIDTH), BF16),
            pltpu.VMEM((PAD, WIDTH), BF16),
            pltpu.VMEM((WIDTH, PAD), BF16),
            pltpu.VMEM((COLS, BLOCK, LANES), BF16),
            pltpu.VMEM((BLOCK, SLOT_ROWS), BF16),
            pltpu.VMEM((SLOT_ROWS, BLOCK), BF16),
            pltpu.VMEM((BLOCK, SLOT_ROWS), BF16),
            pltpu.VMEM((SLOT_ROWS, BLOCK), BF16),
            pltpu.VMEM((SLOT_ROWS, LANES), BF16),
            pltpu.VMEM((SLOT_ROWS, LANES), BF16),
            pltpu.VMEM((SLOT_ROWS, LANES), F32),
            pltpu.VMEM((CHUNK, WIDTH), BF16),
            pltpu.VMEM((YS + 1, XS, 2, MINE, 2 * PAD), BF16),
            pltpu.VMEM((YS + 1, XS, MINE, 2 * PAD), BF16),
            pltpu.VMEM((YS + 1, XS, MINE, 2 * PAD), BF16),
            pltpu.VMEM((YS + 1, XS, MINE, 2 * PAD), BF16),
            pltpu.VMEM((YS + 1, CHUNK, PAD), BF16),
            pltpu.VMEM((MINE, 2 * PAD), F32),
            pltpu.VMEM((ZS, BLOCK, LANES), F32),
            pltpu.VMEM((YS - 1, ZS, BLOCK, LANES), BF16),
            pltpu.VMEM((ZS, YS - 1, BLOCK, LANES), BF16),
            pltpu.VMEM((ZS, BLOCK, LANES), BF16),
            pltpu.VMEM((ZS, BLOCK, LANES), BF16),
            pltpu.VMEM((SLOT_ROWS, LANES), BF16),
            pltpu.VMEM((SLOT_ROWS, LANES), BF16),
            pltpu.VMEM((SLOT_ROWS, LANES), BF16),
            pltpu.VMEM((SLOT_ROWS, LANES), BF16),
            pltpu.VMEM((SLOTS // 2, WIDTH), BF16),
            pltpu.VMEM((2, ROWS, PAD // LANES * SUB, LANES), BF16),
            pltpu.VMEM((2, ROWS, PAD // LANES * SUB, LANES), BF16),
            pltpu.VMEM((2, ROWS, 2 * PAD // LANES * SUB, LANES), BF16),
            pltpu.VMEM((SLOT_ROWS, LANES), BF16),
            pltpu.VMEM((SLOT_ROWS, LANES), BF16),
            sems,
            sems((ZS,)),
            sems,
            sems((YS,)),
            sems((6,)),
            sems((6,)),
            sems((YS + 1,)),
            sems((YS + 1,)),
            sems((YS + 3,)),
            sems((YS + 3,)),
            sems((YS + 3,)),
            sems((YS + 3,)),
            sems,
            sems((ZS,)),
            sems,
            sems,
            pltpu.SemaphoreType.REGULAR,
        ],
        compiler_params=pltpu.CompilerParams(
            collective_id=0, has_side_effects=True, vmem_limit_bytes=64 * 2**20
        ),
    )(teacher, student, gate.T, up.T, down, ids, slots, routes)


def solution(mesh):
    return jax.shard_map(
        shards,
        mesh=mesh,
        in_specs=(
            P("col", "row"),
            P("col", "row"),
            P("row", "col"),
            P("row", "col"),
            P("col", "row"),
            P("col", None),
            P("col", None),
            P("col", None),
        ),
        out_specs=(P("col", "row"), P("col", "row"), P("col", "row")),
        check_vma=False,
    )
```
